128 devices in a mesh: shot: 32 (over z, x, core), line: 4 (over y).
Axes of the slice: x: 4, y: 4, z: 4, core: 2. Of those that a mesh axis runs over, the one named last changes fastest.
Arguments:
- traces: bfloat16 [65536, 2048], P(('shot', 'line')), may hold values from -12 to 12
- targets: bfloat16 [65536, 2048], P(('shot', 'line')), may hold values from -64 to 64
- src_local: int32 [65536], P(('shot', 'line')), may hold values from 0 to 3
- rcv_term: int32 [65536], P(('shot', 'line')), may hold values from 0 to 16383, as said below
- cmp_term: int32 [65536], P(('shot', 'line')), may hold values from 0 to 32767, as said below
- rcv_home: int32 [16384], replicated, may hold values from 0 to 16383, as said below
- cmp_home: int32 [32768], replicated, may hold values from 0 to 32767, as said below
- counts: int32 [128], P(('shot', 'line')), may hold values from 128 to 512, as said below
- src_filters: float32 [512, 128], P(('shot', 'line')), may hold values from -1.75 to 1.75
- rcv_filters: float32 [16384, 128], P(('shot', 'line')), may hold values from -1.75 to 1.75
- cmp_filters: float32 [32768, 128], P(('shot', 'line')), may hold values from -1.75 to 1.75
Outputs:
- src_out: float32 [512, 128], P(('shot', 'line'))
- rcv_out: float32 [16384, 128], P(('shot', 'line'))
- cmp_out: float32 [32768, 128], P(('shot', 'line'))
The draws below stay inside these ranges and needn't reach their ends.
Inputs may be any that keep to these rules, and one draw needn't show every extreme that they name: Receiver row rcv_home[rcv_term[t]] lies on device rcv_home[rcv_term[t]] // 128. Among the 512 trace slots of one device (live or not) at most 8 have receiver rows on any one device; in every draw some device holds the receiver rows of exactly 8 slots of every device. `cmp_term`: likewise for CMP rows with 256 rows a device: at most 8 slots of one device name CMP rows on any one device, and some device is named so by exactly 8 slots of every device. `rcv_home`: A permutation of 0 to 16383. `cmp_home`: A permutation of 0 to 32767. The first counts[d] slots of device d are live; some device is full.
All inputs are finite; a program needn't handle non-finite values.
Results may differ from the reference program's by a relative error of at most 0.0027.
Values sent between devices are 32-bit elements; how exact they have to be, the bound alone decides.
No kernel may reach another device: no remote copies, remote signals or barrier semaphores. Data moves between devices by JAX's collectives and lax.ppermute only.
A program may use at most 64 MiB of HBM per device.

```python
import jax
import jax.numpy as jnp
from jax import lax

TAPS = 128
NS = 2048
TR_DEV = 512
SRC_DEV = 4
RCV_DEV = 128
CMP_DEV = 256
TRACES = 65536
NSRC = 512
NRCV = 16384
NCMP = 32768
CAP = 8
DEVICES = 128


def owner_slots(key, terms_dev):
    star_key, rest_key, place_key = jax.random.split(key, 3)
    star_owner = jax.random.randint(star_key, (), 0, DEVICES).astype(jnp.int32)

    def one_device(device_key):
        first_key, second_key = jax.random.split(device_key)
        others = (jnp.arange(CAP * (DEVICES - 1), dtype=jnp.int32) // CAP + star_owner + 1) % DEVICES
        others = jax.random.permutation(first_key, others)[:TR_DEV - CAP]
        owners = jnp.concatenate([jnp.full((CAP,), star_owner, jnp.int32), others.astype(jnp.int32)])
        return jax.random.permutation(second_key, owners)
    device_keys = jax.random.split(rest_key, DEVICES)
    owners = jax.vmap(one_device)(device_keys)
    place_rows = jax.random.randint(place_key, (DEVICES, TR_DEV), 0, terms_dev).astype(jnp.int32)
    return (owners * terms_dev + place_rows).reshape(-1).astype(jnp.int32)


def term_tables(key, salt, terms_dev, term_total):
    slot_rows = owner_slots(jax.random.fold_in(key, salt), terms_dev)
    home_rows = jax.random.permutation(jax.random.fold_in(key, salt + 1), term_total).astype(jnp.int32)
    inverse = jnp.argsort(home_rows).astype(jnp.int32)
    return (inverse[slot_rows].astype(jnp.int32), home_rows)


def draw_rcv_term(key, part):
    shared = term_tables(key, 101, RCV_DEV, NRCV)
    return shared[0]


def draw_rcv_home(key, part):
    shared = term_tables(key, 101, RCV_DEV, NRCV)
    return shared[1]


def draw_cmp_term(key, part):
    shared = term_tables(key, 201, CMP_DEV, NCMP)
    return shared[0]


def draw_cmp_home(key, part):
    shared = term_tables(key, 201, CMP_DEV, NCMP)
    return shared[1]


def draw_counts(key, part):
    key = jax.random.fold_in(key, 7)
    first_key, second_key = jax.random.split(key)
    counts = jax.random.randint(first_key, (DEVICES,), TR_DEV // 4, TR_DEV + 1)
    full_device = jax.random.randint(second_key, (), 0, DEVICES)
    return jnp.where(jnp.arange(DEVICES) == full_device, TR_DEV, counts).astype(jnp.int32)


def draw_traces(key, part):
    key = jax.random.fold_in(key, 11)
    first_key, second_key = jax.random.split(key)
    base_draw = jax.random.truncated_normal(first_key, -4.0, 4.0, (TRACES, NS), jnp.float32)
    row_scale = jnp.exp(jax.random.uniform(second_key, (TRACES, 1), jnp.float32, jnp.log(0.3), jnp.log(3.0)))
    return (base_draw * row_scale).astype(jnp.bfloat16)


def set_ends(array, rng, low, top_value):
    spot = [jax.random.randint(jax.random.fold_in(rng, axis), (), 0, length) for axis, length in enumerate(array.shape)]
    widest = array.shape.index(max(array.shape))
    neighbour = spot[:widest] + [(spot[widest] + 1) % array.shape[widest]] + spot[widest + 1:]
    return array.at[tuple(spot)].set(low).at[tuple(neighbour)].set(top_value)


def shard_levels(own_key, shape, cuts, smallest, top_value):
    loudness, own = 1.0, jax.random.fold_in(own_key, 6)
    for dim, blocks in cuts:
        steps = jnp.exp(jax.random.uniform(jax.random.fold_in(own, dim), (blocks,), jnp.float32, smallest / len(cuts), top_value / len(cuts)))
        loudness = loudness * jnp.repeat(steps, shape[dim] // blocks).reshape([-1 if axis == dim else 1 for axis in range(len(shape))])
    return loudness


def gaussian(key, shape, deviation, most, cuts=(), kind=jnp.bfloat16):
    result = deviation * jax.random.normal(key, shape, jnp.float32)
    if cuts:
        result = result * shard_levels(key, shape, cuts, -0.22, 0.18)
    return jnp.clip(result, -most, most).astype(kind)


def setup_inputs(seed: int = 0) -> dict:
    arg_keys = jax.random.split(jax.random.key(seed), 12)
    traces = draw_traces(jax.random.fold_in(arg_keys[11], 71), 0)
    targets = gaussian(arg_keys[1], (TRACES, NS), 12.0, 64.0, ((0, 128),))
    src_local = set_ends(jax.random.randint(arg_keys[2], (TRACES,), 0, SRC_DEV), jax.random.fold_in(arg_keys[2], 1), 0, SRC_DEV - 1).astype(jnp.int32)
    rcv_term = draw_rcv_term(jax.random.fold_in(arg_keys[11], 71), 0)
    cmp_term = draw_cmp_term(jax.random.fold_in(arg_keys[11], 71), 0)
    rcv_home = draw_rcv_home(jax.random.fold_in(arg_keys[11], 71), 0)
    cmp_home = draw_cmp_home(jax.random.fold_in(arg_keys[11], 71), 0)
    counts = draw_counts(jax.random.fold_in(arg_keys[11], 71), 0)
    src_filters = gaussian(arg_keys[8], (NSRC, TAPS), 0.3, 1.75, ((0, 128),), jnp.float32)
    rcv_filters = gaussian(arg_keys[9], (NRCV, TAPS), 0.3, 1.75, ((0, 128),), jnp.float32)
    cmp_filters = gaussian(arg_keys[10], (NCMP, TAPS), 0.3, 1.75, ((0, 128),), jnp.float32)
    return dict(traces=traces, targets=targets, src_local=src_local, rcv_term=rcv_term, cmp_term=cmp_term, rcv_home=rcv_home, cmp_home=cmp_home, counts=counts, src_filters=src_filters, rcv_filters=rcv_filters, cmp_filters=cmp_filters)


def trace_terms(pieces):
    trace_data, target_data, filter_rows, live_rows = pieces
    row_width = NS + TAPS
    signal = trace_data.astype(jnp.float32)
    signal_spectrum = jnp.fft.rfft(signal, n=row_width, axis=1)
    filter_spectrum = jnp.fft.rfft(filter_rows.astype(jnp.float32), n=row_width, axis=1)
    model_trace = jnp.fft.irfft(signal_spectrum * filter_spectrum, n=row_width, axis=1)[:, :NS]
    difference = model_trace - target_data.astype(jnp.float32)
    misfit = jnp.where(live_rows[:, None], difference, jnp.zeros_like(difference)).astype(jnp.bfloat16)
    misfit_spectrum = jnp.fft.rfft(misfit.astype(jnp.float32), n=row_width, axis=1)
    grad_trace = jnp.fft.irfft(misfit_spectrum * jnp.conj(signal_spectrum), n=row_width, axis=1)[:, :TAPS]
    squares = jnp.sum(signal * signal, axis=1)
    power = jnp.where(live_rows, squares, jnp.zeros_like(squares))
    return grad_trace, power


def reference(traces, targets, src_local, rcv_term, cmp_term, rcv_home, cmp_home, counts, src_filters, rcv_filters, cmp_filters):
    slot_index = jnp.arange(TRACES, dtype=jnp.int32)
    device_of = slot_index // TR_DEV
    src_slot = (device_of * SRC_DEV + src_local).astype(jnp.int32)
    rcv_slot = rcv_home[rcv_term].astype(jnp.int32)
    cmp_slot = cmp_home[cmp_term].astype(jnp.int32)
    live_mask = (slot_index % TR_DEV) < counts[device_of]
    mixed_filters = ((src_filters[src_slot] + rcv_filters[rcv_slot]) + cmp_filters[cmp_slot]).astype(jnp.bfloat16)
    grad_trace, power = lax.map(trace_terms, (
        traces.reshape(DEVICES, TR_DEV, NS),
        targets.reshape(DEVICES, TR_DEV, NS),
        mixed_filters.reshape(DEVICES, TR_DEV, TAPS),
        live_mask.reshape(DEVICES, TR_DEV)))
    grad_trace = grad_trace.reshape(TRACES, TAPS)
    power = power.reshape(TRACES)

    def settle(filter_table, slots, term_count):
        grad_sum = jax.ops.segment_sum(grad_trace, slots, num_segments=term_count)
        power_sum = jax.ops.segment_sum(power, slots, num_segments=term_count)
        return filter_table - 0.5 * grad_sum / jnp.maximum(power_sum, 1.0)[:, None]

    return (settle(src_filters, src_slot, NSRC),
            settle(rcv_filters, rcv_slot, NRCV),
            settle(cmp_filters, cmp_slot, NCMP))
```

```python
import jax
import jax.numpy as jnp
import numpy as np
import ml_dtypes
from jax import lax
from jax.experimental import pallas as pl
from jax.experimental.pallas import tpu as pltpu
from jax.sharding import PartitionSpec as P

AXES = ("shot", "line")
DEVS = 128
ROWS = 512
NS = 2048
TAPS = 128
CAP = 8
PAIR = 2 * CAP
SLOTS = DEVS * PAIR
RCV = 128
CMP = 256
SRC = 4
WIN = 256
BLOCKS = NS // TAPS
ROWBLK = 128
step_size = 0.5
f32, bf16, i32 = jnp.float32, jnp.bfloat16, jnp.int32
NT = (((1,), (1,)), ((), ()))
MIB = 1024 * 1024


def split_pair(matrix):
    high = matrix.astype(ml_dtypes.bfloat16)
    low = (matrix - high.astype(np.float64)).astype(ml_dtypes.bfloat16)
    return high, low


def make_tables():
    angle = 2.0 * np.pi * (np.arange(TAPS) + 0.5) / WIN
    place = np.arange(WIN)
    phase = place[:, None] * angle[None, :]
    forward = np.concatenate([np.cos(phase), -np.sin(phase)], axis=1)
    inverse = forward.T / TAPS
    lag_phase = np.arange(TAPS)[:, None] * angle[None, :]
    even = 2.0 * np.cos(lag_phase)
    even[0] = 1.0
    f_high, f_low = split_pair(forward)
    d_pair = np.concatenate(split_pair(forward[:TAPS]), axis=0)
    e_pair = np.concatenate(split_pair(forward[TAPS:]), axis=0)
    i_pair = np.concatenate(split_pair(inverse[:, :TAPS]), axis=1)
    c_pair = np.concatenate(split_pair(even), axis=1)
    tail = split_pair(inverse[:, TAPS:] @ forward[TAPS:])[0]
    f_pair = np.concatenate([f_high, f_low], axis=0)
    return dict(f=f_pair, d=d_pair, e=e_pair, i=i_pair, c=c_pair, tail=tail)


def two(values):
    high = values.astype(bf16)
    low = (values - high.astype(f32)).astype(bf16)
    return high, low


def mm(a, b):
    return jnp.dot(a, b, preferred_element_type=f32)


def iota(shape, dim):
    return lax.broadcasted_iota(i32, shape, dim)


def as_bf16(mask):
    return mask.astype(f32).astype(bf16)


def fine_mm(values, pair):
    width = pair.shape[1] // 2
    high, low = two(values)
    both = mm(high, pair)
    return both[:, :width] + (both[:, width:] + mm(low, pair[:, :width]))


def plan_kernel(count_ref, rterm_ref, cterm_ref, rhome_ref, chome_ref, traces_hbm,
                pay_ref, slot_ref, tbuf, sems):
    copies = []
    for j in range(4):
        part = pl.ds(j * 128, 128)
        copies.append(pltpu.make_async_copy(traces_hbm.at[part], tbuf.at[part], sems.at[j]))
        copies[-1].start()
    before_mask = as_bf16(iota((ROWS, ROWS), 0) < iota((ROWS, ROWS), 1))

    def look_up(term, home, bits):
        high, low = term >> 7, term & 127
        owner_t = jnp.transpose((home >> bits).astype(f32)).astype(bf16)
        place_t = jnp.transpose((home & (2 ** bits - 1)).astype(f32)).astype(bf16)
        pick_high = as_bf16(iota((home.shape[0], ROWS), 0) == high)
        pick_low = iota((128, ROWS), 0) == low
        owner = jnp.sum(jnp.where(pick_low, mm(owner_t, pick_high), 0.0), axis=0, keepdims=True)
        place = jnp.sum(jnp.where(pick_low, mm(place_t, pick_high), 0.0), axis=0, keepdims=True)
        mine = iota((DEVS, ROWS), 0) == owner.astype(i32)
        mine16 = as_bf16(mine)
        before = mm(mine16, before_mask)
        rank = jnp.sum(jnp.where(mine, before, 0.0), axis=0, keepdims=True)
        return owner, place, rank, mine16

    r_owner, r_place, r_rank, r_mine = look_up(rterm_ref[...], rhome_ref[...], 7)
    c_owner, c_place, c_rank, c_mine = look_up(cterm_ref[...], chome_ref[...], 8)
    live = (iota((1, ROWS), 1) < count_ref[0]).astype(f32)
    r_slot = r_owner * PAIR + r_rank
    c_slot = c_owner * PAIR + (c_rank + CAP)
    powers = []
    for j in range(4):
        copies[j].wait()
        total = jnp.zeros((128, 128), f32)
        for b in range(BLOCKS):
            x = tbuf[j * 128:(j + 1) * 128, b * 128:(b + 1) * 128].astype(f32)
            total = total + x * x
        powers.append(jnp.sum(jnp.transpose(total), axis=0, keepdims=True))
    power = jnp.concatenate(powers, axis=1) * live
    p_high, p_low = two(power)
    p_high, p_low = p_high.astype(f32), p_low.astype(f32)
    line = iota((2 * PAIR, ROWS), 0).astype(f32)

    def weights(rank, place):
        at_place = jnp.where(line == rank, place, 0.0)
        here = line == rank + PAIR
        return ((at_place + jnp.where(here, p_high, 0.0)).astype(bf16),
                jnp.where(here, p_low, 0.0).astype(bf16))

    pay = jnp.zeros((DEVS, 2 * PAIR), f32)
    for mine, rank, place in ((r_mine, r_rank, r_place), (c_mine, c_rank + CAP, c_place)):
        for weight in weights(rank, place):
            pay = pay + lax.dot_general(mine, weight, NT, preferred_element_type=f32)
    pay_ref[...] = pay
    slot_ref[...] = jnp.concatenate(
        [r_slot, c_slot, live, power, jnp.zeros((4, ROWS), f32)], axis=0)


def pick_kernel(got_ref, rcv_ref, cmp_ref, out_ref):
    got = got_ref[...].astype(bf16)
    table = jnp.concatenate([rcv_ref[...], cmp_ref[...]], axis=0)
    pair = jnp.concatenate(two(table), axis=1)
    chunk = 512
    ones = jnp.ones((2 * PAIR, 128), bf16)
    for c in range(SLOTS // chunk):
        spread = as_bf16((iota((chunk, DEVS), 0) + c * chunk) >> 4 == iota((chunk, DEVS), 1))
        line = mm(spread, got)
        keep = iota((chunk, 2 * PAIR), 1) == (iota((chunk, 2 * PAIR), 0) & (PAIR - 1))
        place = mm(jnp.where(keep, line, 0.0).astype(bf16), ones).astype(i32)
        place = place + ((iota((chunk, 128), 0) & CAP) << 4)
        lane = iota((chunk, 128), 1)
        pick = jnp.concatenate([as_bf16(place == lane + k * 128) for k in range(3)], axis=1)
        both = mm(pick, pair)
        out_ref[c * chunk:(c + 1) * chunk, :] = both[:, :TAPS] + both[:, TAPS:]


def lags_kernel(after_ref, traces_ref, targets_ref, f_ref, e_ref, i_ref, c_ref, d_ref,
                even_ref, base_ref, last_ref):
    f_high, f_low = f_ref[:WIN, :], f_ref[WIN:, :]
    e_pair = e_ref[...]
    own = jnp.zeros((ROWBLK, WIN), f32)
    cross = jnp.zeros((ROWBLK, WIN), f32)
    for b in range(BLOCKS):
        now = traces_ref[:, b * 128:(b + 1) * 128]
        goal = targets_ref[:, b * 128:(b + 1) * 128]
        u = mm(jnp.concatenate([now, now], axis=1), e_pair)
        v = mm(jnp.concatenate([goal, goal], axis=1), e_pair)
        if b == 0:
            x = u
        else:
            window = traces_ref[:, (b - 1) * 128:(b + 1) * 128]
            x = mm(window, f_high) + mm(window, f_low)
        xr, xi = x[:, :TAPS], x[:, TAPS:]
        flip = jnp.concatenate([xi, -xr], axis=1)
        for_re = jnp.concatenate([xr, xr], axis=1)
        ur, ui = u[:, :TAPS], u[:, TAPS:]
        vr, vi = v[:, :TAPS], v[:, TAPS:]
        own = own + jnp.concatenate([xr * ur + xi * ui, xr * ui - xi * ur], axis=1)
        cross = cross + jnp.concatenate([xr * vr + xi * vi, xr * vi - xi * vr], axis=1)
    i_pair = i_ref[...]
    even_ref[...] = fine_mm(fine_mm(own, i_pair), c_ref[...])
    base_ref[...] = fine_mm(cross, i_pair)
    final = traces_ref[:, (BLOCKS - 1) * 128:]
    last_ref[...] = mm(jnp.concatenate([final, final], axis=1), d_ref[...])


def books_kernel(got_ref, slot_ref, srcloc_ref, place_ref, energy_ref, col_ref):
    got = jnp.concatenate([got_ref[...], jnp.zeros((DEVS, 128 - 2 * PAIR), f32)], axis=1)
    turned = jnp.transpose(got)[:2 * PAIR]
    first = turned.astype(bf16)
    rest = turned - first.astype(f32)
    second = rest.astype(bf16)
    third = (rest - second.astype(f32)).astype(bf16)
    q = iota((DEVS, SLOTS), 1)
    spread = as_bf16((q >> 4) == iota((DEVS, SLOTS), 0))
    wide = mm(first, spread) + (mm(second, spread) + mm(third, spread))
    line = iota((PAIR, SLOTS), 0)
    slot = iota((PAIR, SLOTS), 1) & (PAIR - 1)
    place = jnp.sum(jnp.where(line == slot, wide[:PAIR], 0.0), axis=0, keepdims=True)
    power = jnp.sum(jnp.where(line == slot, wide[PAIR:], 0.0), axis=0, keepdims=True)
    place = place.astype(i32) + ((iota((1, SLOTS), 1) & CAP) << 4)
    place_ref[...] = jnp.broadcast_to(place, (8, SLOTS))
    for c in range(3):
        rows = iota((128, SLOTS), 0) + c * 128
        energy = jnp.sum(jnp.where(rows == place, power, 0.0), axis=1, keepdims=True)
        energy_ref[c * 128:(c + 1) * 128, :] = jnp.broadcast_to(
            step_size / jnp.maximum(energy, 1.0), (128, 128))
    lines = jnp.concatenate(
        [slot_ref[...], srcloc_ref[...].astype(f32), jnp.zeros((128 - 9, ROWS), f32)], axis=0)
    for j in range(4):
        col_ref[j * 128:(j + 1) * 128, :] = jnp.transpose(lines[:, j * 128:(j + 1) * 128])


def grad_kernel(fetched_ref, col_ref, slot_ref, srcloc_ref, src_ref, even_ref, base_ref,
                last_ref, d_ref, tail_ref, i_ref, out_ref, src_out_ref):
    col = col_ref[...]
    r_slot = col[:, 0:1].astype(i32)
    c_slot = col[:, 1:2].astype(i32)
    live = col[:, 2:3]
    src_local = col[:, 8:9]
    src = src_ref[...]
    mixed = jnp.zeros((ROWS, TAPS), f32)
    for s in range(SRC):
        mixed = jnp.where(src_local == float(s), src[s:s + 1, :], mixed)
    width = 256
    lane = iota((ROWS, width), 1)
    both = jnp.zeros((ROWS, 2 * TAPS), f32)
    for k in range(SLOTS // width):
        at = lane + k * width
        pick = as_bf16((at == r_slot) | (at == c_slot))
        rows = jnp.concatenate(two(fetched_ref[k * width:(k + 1) * width, :]), axis=1)
        both = both + mm(pick, rows)
    mixed = (mixed + (both[:, :TAPS] + both[:, TAPS:])).astype(bf16)
    h = mm(jnp.concatenate([mixed, mixed], axis=1), d_ref[...])
    hr, hi = h[:, :TAPS], h[:, TAPS:]
    xr, xi = last_ref[:, :TAPS], last_ref[:, TAPS:]
    past = jnp.concatenate([xr * hr - xi * hi, xr * hi + xi * hr], axis=1)
    m = mm(past.astype(bf16), tail_ref[...])
    mr, mi = m[:, :TAPS], m[:, TAPS:]
    even = even_ref[...]
    spectrum = jnp.concatenate(
        [even * hr - (xr * mr + xi * mi), even * hi - (xr * mi - xi * mr)], axis=1)
    grad = (fine_mm(spectrum, i_ref[...]) - base_ref[...]) * live
    rows = jnp.concatenate(two(grad), axis=1)
    lines = slot_ref[...]
    r_line, c_line, power = lines[0:1].astype(i32), lines[1:2].astype(i32), lines[3:4]
    chunk = 512
    for k in range(SLOTS // chunk):
        at = iota((chunk, ROWS), 0) + k * chunk
        place = as_bf16((at == r_line) | (at == c_line))
        both = mm(place, rows)
        out_ref[k * chunk:(k + 1) * chunk, :] = both[:, :TAPS] + both[:, TAPS:]
    mine = iota((8, ROWS), 0) == srcloc_ref[...]
    both = mm(as_bf16(mine), rows)
    energy = jnp.sum(jnp.where(mine, power, 0.0), axis=1, keepdims=True)
    change = step_size * (both[:, :TAPS] + both[:, TAPS:]) / jnp.maximum(energy, 1.0)
    src_out_ref[...] = src - change[:SRC]


def settle_kernel(grads_ref, place_ref, energy_ref, rcv_ref, cmp_ref, rcv_out_ref, cmp_out_ref):
    place = place_ref[0:1, :]
    total = jnp.zeros((RCV + CMP, 2 * TAPS), f32)
    width = 256
    for k in range(SLOTS // width):
        rows = jnp.concatenate(two(grads_ref[k * width:(k + 1) * width, :]), axis=1)
        pick = as_bf16(iota((RCV + CMP, width), 0) == place[:, k * width:(k + 1) * width])
        total = total + mm(pick, rows)
    change = (total[:, :TAPS] + total[:, TAPS:]) * energy_ref[...]
    rcv_out_ref[...] = rcv_ref[...] - change[:RCV]
    cmp_out_ref[...] = cmp_ref[...] - change[RCV:]


def shape(*dims, dtype=f32):
    return jax.ShapeDtypeStruct(dims, dtype)


VM = pl.BlockSpec(memory_space=pltpu.VMEM)
SM = pl.BlockSpec(memory_space=pltpu.SMEM)
params = pltpu.CompilerParams(vmem_limit_bytes=40 * MIB)


def body(traces, targets, src_local, rcv_term, cmp_term, rcv_home, cmp_home, counts,
         src_filters, rcv_filters, cmp_filters):
    tables = {name: jnp.asarray(value) for name, value in make_tables().items()}
    src_line = src_local.reshape(1, ROWS)
    pay, slot_lines = pl.pallas_call(
        plan_kernel,
        out_shape=(shape(DEVS, 2 * PAIR), shape(8, ROWS)),
        in_specs=[SM, VM, VM, VM, VM, pl.BlockSpec(memory_space=pl.ANY)],
        out_specs=(VM, VM),
        scratch_shapes=[pltpu.VMEM((ROWS, NS), bf16), pltpu.SemaphoreType.DMA((4,))],
        compiler_params=params,
        name="plan",
    )(counts, rcv_term.reshape(1, ROWS), cmp_term.reshape(1, ROWS),
      rcv_home.reshape(-1, 128), cmp_home.reshape(-1, 128), traces)
    got = lax.all_to_all(pay, AXES, split_axis=0, concat_axis=0, tiled=True)
    values = pl.pallas_call(
        pick_kernel,
        out_shape=shape(SLOTS, TAPS),
        in_specs=[VM] * 3, out_specs=VM,
        compiler_params=params,
        name="pick",
    )(got, rcv_filters, cmp_filters)
    fetched = lax.all_to_all(values.reshape(DEVS, PAIR, TAPS), AXES, split_axis=0, concat_axis=0,
                             tiled=True).reshape(SLOTS, TAPS)

    def whole(array):
        return pl.BlockSpec(array.shape, lambda i: (0, 0))

    def blk(width):
        return pl.BlockSpec((ROWBLK, width), lambda i: (i, 0))

    even, base, last = pl.pallas_call(
        lags_kernel,
        grid=(ROWS // ROWBLK,),
        out_shape=(shape(ROWS, TAPS), shape(ROWS, TAPS), shape(ROWS, WIN)),
        in_specs=[pl.BlockSpec((8, 2 * PAIR), lambda i: (0, 0)), blk(NS), blk(NS)]
        + [whole(tables[n]) for n in "feicd"],
        out_specs=(blk(TAPS), blk(TAPS), blk(WIN)),
        compiler_params=params,
        cost_estimate=pl.CostEstimate(flops=5 * 10 ** 9, bytes_accessed=5 * 10 ** 6,
                                      transcendentals=0),
        name="lags",
    )(got, traces, targets, *[tables[n] for n in "feicd"])
    place, energy, cols = pl.pallas_call(
        books_kernel,
        out_shape=(shape(8, SLOTS, dtype=i32), shape(RCV + CMP, 128), shape(ROWS, 128)),
        in_specs=[VM] * 3, out_specs=(VM,) * 3,
        compiler_params=params,
        name="books",
    )(got, slot_lines, src_line)
    send, src_out = pl.pallas_call(
        grad_kernel,
        out_shape=(shape(SLOTS, TAPS), shape(SRC, TAPS)),
        in_specs=[VM] * 11, out_specs=(VM, VM),
        compiler_params=params,
        name="grad",
    )(fetched, cols, slot_lines, src_line, src_filters, even, base, last,
      tables["d"], tables["tail"], tables["i"])
    back = lax.all_to_all(send.reshape(DEVS, PAIR, TAPS), AXES, split_axis=0, concat_axis=0,
                          tiled=True).reshape(SLOTS, TAPS)
    rcv_out, cmp_out = pl.pallas_call(
        settle_kernel,
        out_shape=(shape(RCV, TAPS), shape(CMP, TAPS)),
        in_specs=[VM] * 5, out_specs=(VM, VM),
        compiler_params=params,
        name="settle",
    )(back, place, energy, rcv_filters, cmp_filters)
    return src_out, rcv_out, cmp_out


def solution(mesh):
    rows = P(AXES, None)
    flat = P(AXES)
    return jax.shard_map(
        body,
        mesh=mesh,
        in_specs=(rows, rows, flat, flat, flat, P(), P(), flat, rows, rows, rows),
        out_specs=(rows, rows, rows),
        check_vma=False,
    )
```

```python
import jax
import jax.numpy as jnp
import numpy as np
import ml_dtypes
from jax import lax
from jax.experimental import pallas as pl
from jax.experimental.pallas import tpu as pltpu
from jax.sharding import PartitionSpec as P

AXES = ("shot", "line")
DEVS = 128
ROWS = 512
NS = 2048
TAPS = 128
CAP = 8
PAIR = 2 * CAP
SLOTS = DEVS * PAIR
RCV = 128
CMP = 256
SRC = 4
WIN = 256
BLOCKS = NS // TAPS
ROWBLK = 128
step_size = 0.5
f32, bf16, i32 = jnp.float32, jnp.bfloat16, jnp.int32
NT = (((1,), (1,)), ((), ()))
MIB = 1024 * 1024


def split_pair(matrix):
    high = matrix.astype(ml_dtypes.bfloat16)
    low = (matrix - high.astype(np.float64)).astype(ml_dtypes.bfloat16)
    return high, low


def make_tables():
    angle = 2.0 * np.pi * (np.arange(TAPS) + 0.5) / WIN
    place = np.arange(WIN)
    phase = place[:, None] * angle[None, :]
    forward = np.concatenate([np.cos(phase), -np.sin(phase)], axis=1)
    inverse = forward.T / TAPS
    lag_phase = np.arange(TAPS)[:, None] * angle[None, :]
    even = 2.0 * np.cos(lag_phase)
    even[0] = 1.0
    f_high, f_low = split_pair(forward)
    d_pair = np.concatenate(split_pair(forward[:TAPS]), axis=0)
    e_pair = np.concatenate(split_pair(forward[TAPS:]), axis=0)
    i_pair = np.concatenate(split_pair(inverse[:, :TAPS]), axis=1)
    c_pair = np.concatenate(split_pair(even), axis=1)
    tail = split_pair(inverse[:, TAPS:] @ forward[TAPS:])[0]
    f_pair = np.concatenate([f_high, f_low], axis=0)
    return dict(f=f_pair, d=d_pair, e=e_pair, i=i_pair, c=c_pair, tail=tail)


def two(values):
    high = values.astype(bf16)
    low = (values - high.astype(f32)).astype(bf16)
    return high, low


def mm(a, b):
    return jnp.dot(a, b, preferred_element_type=f32)


def iota(shape, dim):
    return lax.broadcasted_iota(i32, shape, dim)


def as_bf16(mask):
    return mask.astype(f32).astype(bf16)


def fine_mm(values, pair):
    width = pair.shape[1] // 2
    high, low = two(values)
    both = mm(high, pair)
    return both[:, :width] + (both[:, width:] + mm(low, pair[:, :width]))


def fetch(hbm_refs, vmem_refs, sems):
    copies = [pltpu.make_async_copy(src, dst, sems.at[j])
              for j, (src, dst) in enumerate(zip(hbm_refs, vmem_refs))]
    for copy in copies:
        copy.start()
    return copies


def plan_kernel(count_ref, rterm_hbm, cterm_hbm, rhome_hbm, chome_hbm, traces_hbm,
                pay_ref, slot_hbm, rterm_ref, cterm_ref, rhome_ref, chome_ref, tbuf, slot_ref, sems):
    parts = [pl.ds(j * 128, 128) for j in range(4)]
    copies = fetch([rterm_hbm, cterm_hbm, rhome_hbm, chome_hbm] + [traces_hbm.at[p] for p in parts],
                   [rterm_ref, cterm_ref, rhome_ref, chome_ref] + [tbuf.at[p] for p in parts], sems)
    before_mask = as_bf16(iota((ROWS, ROWS), 0) < iota((ROWS, ROWS), 1))

    def look_up(term, home, bits):
        high, low = term >> 7, term & 127
        owner_t = jnp.transpose((home >> bits).astype(f32)).astype(bf16)
        place_t = jnp.transpose((home & (2 ** bits - 1)).astype(f32)).astype(bf16)
        pick_high = as_bf16(iota((home.shape[0], ROWS), 0) == high)
        pick_low = iota((128, ROWS), 0) == low
        owner = jnp.sum(jnp.where(pick_low, mm(owner_t, pick_high), 0.0), axis=0, keepdims=True)
        place = jnp.sum(jnp.where(pick_low, mm(place_t, pick_high), 0.0), axis=0, keepdims=True)
        mine = iota((DEVS, ROWS), 0) == owner.astype(i32)
        mine16 = as_bf16(mine)
        before = mm(mine16, before_mask)
        rank = jnp.sum(jnp.where(mine, before, 0.0), axis=0, keepdims=True)
        return owner, place, rank, mine16

    for copy in copies[:4]:
        copy.wait()
    r_owner, r_place, r_rank, r_mine = look_up(rterm_ref[...], rhome_ref[...], 7)
    c_owner, c_place, c_rank, c_mine = look_up(cterm_ref[...], chome_ref[...], 8)
    live = (iota((1, ROWS), 1) < count_ref[0]).astype(f32)
    r_slot = r_owner * PAIR + r_rank
    c_slot = c_owner * PAIR + (c_rank + CAP)
    powers = []
    for j in range(4):
        copies[4 + j].wait()
        total = jnp.zeros((128, 128), f32)
        for b in range(BLOCKS):
            x = tbuf[j * 128:(j + 1) * 128, b * 128:(b + 1) * 128].astype(f32)
            total = total + x * x
        powers.append(jnp.sum(jnp.transpose(total), axis=0, keepdims=True))
    power = jnp.concatenate(powers, axis=1) * live
    slot_ref[...] = jnp.concatenate(
        [r_slot, c_slot, live, power, jnp.zeros((4, ROWS), f32)], axis=0)
    save = pltpu.make_async_copy(slot_ref, slot_hbm, sems.at[8])
    save.start()
    p_high, p_low = two(power)
    p_high, p_low = p_high.astype(f32), p_low.astype(f32)
    line = iota((2 * PAIR, ROWS), 0).astype(f32)

    def weights(rank, place):
        at_place = jnp.where(line == rank, place, 0.0)
        here = line == rank + PAIR
        return ((at_place + jnp.where(here, p_high, 0.0)).astype(bf16),
                jnp.where(here, p_low, 0.0).astype(bf16))

    pay = jnp.zeros((DEVS, 2 * PAIR), f32)
    for mine, rank, place in ((r_mine, r_rank, r_place), (c_mine, c_rank + CAP, c_place)):
        for weight in weights(rank, place):
            pay = pay + lax.dot_general(mine, weight, NT, preferred_element_type=f32)
    pay_ref[...] = pay
    save.wait()


def pick_kernel(got_ref, rcv_ref, cmp_ref, out_hbm, out_ref, sem):
    got = got_ref[...].astype(i32)
    rcv_pair = jnp.concatenate(two(rcv_ref[...]), axis=1)
    cmp_pair = jnp.concatenate(two(cmp_ref[...]), axis=1)
    for s in range(PAIR):
        pair = rcv_pair if s < CAP else cmp_pair
        rows = pair.shape[0]
        pick = as_bf16(iota((DEVS, rows), 1) == got[:, s:s + 1])
        both = mm(pick, pair)
        out_ref[pl.ds(s, DEVS, stride=PAIR), :] = both[:, :TAPS] + both[:, TAPS:]
    save = pltpu.make_async_copy(out_ref, out_hbm, sem)
    save.start()
    save.wait()


def lags_kernel(count_ref, after_ref, traces_ref, targets_ref, f_ref, e_ref, i_ref, c_ref, d_ref,
                even_ref, base_ref, last_ref):
    f_high, f_low = f_ref[:WIN, :], f_ref[WIN:, :]
    e_pair = e_ref[...]
    own = jnp.zeros((ROWBLK, WIN), f32)
    cross = jnp.zeros((ROWBLK, WIN), f32)
    for b in range(BLOCKS):
        now = traces_ref[:, b * 128:(b + 1) * 128]
        goal = targets_ref[:, b * 128:(b + 1) * 128]
        u = mm(jnp.concatenate([now, now], axis=1), e_pair)
        v = mm(jnp.concatenate([goal, goal], axis=1), e_pair)
        if b == 0:
            x = u
        else:
            window = traces_ref[:, (b - 1) * 128:(b + 1) * 128]
            x = mm(window, f_high) + mm(window, f_low)
        xr, xi = x[:, :TAPS], x[:, TAPS:]
        ur, ui = u[:, :TAPS], u[:, TAPS:]
        vr, vi = v[:, :TAPS], v[:, TAPS:]
        own = own + jnp.concatenate([xr * ur + xi * ui, xr * ui - xi * ur], axis=1)
        cross = cross + jnp.concatenate([xr * vr + xi * vi, xr * vi - xi * vr], axis=1)
    i_pair = i_ref[...]
    row = iota((ROWBLK, TAPS), 0) + pl.program_id(0) * ROWBLK
    live = row < count_ref[0]
    even_ref[...] = jnp.where(live, fine_mm(fine_mm(own, i_pair), c_ref[...]), 0.0)
    base_ref[...] = jnp.where(live, fine_mm(cross, i_pair), 0.0)
    final = traces_ref[:, (BLOCKS - 1) * 128:]
    last = mm(jnp.concatenate([final, final], axis=1), d_ref[...])
    last_ref[...] = jnp.where(jnp.concatenate([live, live], axis=1), last, 0.0)


def books_kernel(got_ref, slot_ref, srcloc_ref, src_ref,
                 settle_ref, energy_ref, rcol_ref, ccol_ref, line_ref, shot_ref, scale_ref):
    got = jnp.concatenate([got_ref[...], jnp.zeros((DEVS, 128 - 2 * PAIR), f32)], axis=1)
    turned = jnp.transpose(got)[:2 * PAIR]
    first = turned.astype(bf16)
    rest = turned - first.astype(f32)
    second = rest.astype(bf16)
    third = (rest - second.astype(f32)).astype(bf16)
    q = iota((DEVS, SLOTS), 1)
    spread = as_bf16((q >> 4) == iota((DEVS, SLOTS), 0))
    wide = mm(first, spread) + (mm(second, spread) + mm(third, spread))
    line = iota((PAIR, SLOTS), 0)
    slot = iota((PAIR, SLOTS), 1) & (PAIR - 1)
    place = jnp.sum(jnp.where(line == slot, wide[:PAIR], 0.0), axis=0, keepdims=True)
    power = jnp.sum(jnp.where(line == slot, wide[PAIR:], 0.0), axis=0, keepdims=True)
    place = place.astype(i32) + ((iota((1, SLOTS), 1) & CAP) << 4)
    for c in range(3):
        rows = iota((128, SLOTS), 0) + c * 128
        settle_ref[c * 128:(c + 1) * 128, :] = as_bf16(rows == place)
        energy = jnp.sum(jnp.where(rows == place, power, 0.0), axis=1, keepdims=True)
        energy_ref[c * 128:(c + 1) * 128, :] = jnp.broadcast_to(
            step_size / jnp.maximum(energy, 1.0), (128, 128))
    lines = jnp.concatenate(
        [slot_ref[...], srcloc_ref[...].astype(f32), jnp.zeros((128 - 9, ROWS), f32)], axis=0)
    src = src_ref[...]
    for j in range(4):
        part = slice(j * 128, (j + 1) * 128)
        col = jnp.transpose(lines[:, part])
        rcol_ref[part, :] = jnp.broadcast_to(col[:, 0:1].astype(i32), (128, 128)).astype(jnp.int16)
        ccol_ref[part, :] = jnp.broadcast_to(col[:, 1:2].astype(i32), (128, 128)).astype(jnp.int16)
        src_rows = jnp.zeros((128, TAPS), f32)
        for s in range(SRC):
            src_rows = jnp.where(col[:, 8:9] == float(s), src[s:s + 1, :], src_rows)
        shot_ref[part, :] = src_rows
    for j in range(2):
        line_ref[16 * j:16 * (j + 1), :] = jnp.broadcast_to(
            slot_ref[j:j + 1, :].astype(i32), (16, ROWS)).astype(jnp.int16)
    mine = iota((8, ROWS), 0) == srcloc_ref[...]
    energy = jnp.sum(jnp.where(mine, slot_ref[3:4, :], 0.0), axis=1, keepdims=True)
    scale_ref[:8, :] = jnp.broadcast_to(step_size / jnp.maximum(energy, 1.0), (8, TAPS))
    scale_ref[8:, :] = jnp.concatenate([src, jnp.zeros((8 - SRC, TAPS), f32)], axis=0)


def one_hot16(at, first, second):
    ones = jnp.ones(at.shape, bf16)
    return jnp.where((at == first) | (at == second), ones, jnp.zeros(at.shape, bf16))


def grad_kernel(*refs):
    hbm, (out_hbm, src_out_ref) = refs[:13], refs[13:15]
    vmem, out_ref, sems = refs[15:28], refs[28], refs[29]
    chunk = 256
    chunks = SLOTS // chunk
    parts = [pl.ds(k * chunk, chunk) for k in range(chunks)]
    sources = list(hbm[:2]) + [hbm[2].at[p] for p in parts] + list(hbm[3:])
    targets = list(vmem[:2]) + [vmem[2].at[p] for p in parts] + list(vmem[3:])
    copies = fetch(sources, targets, sems)
    (rcol_ref, ccol_ref, fetched_ref, shot_ref, d_ref, last_ref, tail_ref, even_ref, i_ref, base_ref,
     line_ref, srcloc_ref, scale_src_ref) = vmem
    pieces, others = copies[2:2 + chunks], copies[2 + chunks:]
    lane = lax.broadcasted_iota(jnp.int16, (ROWS, 128), 1)
    copies[0].wait()
    copies[1].wait()
    rcol, ccol = rcol_ref[...], ccol_ref[...]
    both = jnp.zeros((ROWS, 2 * TAPS), f32)
    for k in range(chunks):
        pick = jnp.concatenate(
            [one_hot16(lane + jnp.int16(k * chunk + j * 128), rcol, ccol) for j in range(chunk // 128)],
            axis=1)
        pieces[k].wait()
        rows = jnp.concatenate(two(fetched_ref[k * chunk:(k + 1) * chunk, :]), axis=1)
        both = both + mm(pick, rows)
    for copy in others:
        copy.wait()
    mixed = (shot_ref[...] + (both[:, :TAPS] + both[:, TAPS:])).astype(bf16)
    h = mm(jnp.concatenate([mixed, mixed], axis=1), d_ref[...])
    hr, hi = h[:, :TAPS], h[:, TAPS:]
    xr, xi = last_ref[:, :TAPS], last_ref[:, TAPS:]
    past = jnp.concatenate([xr * hr - xi * hi, xr * hi + xi * hr], axis=1)
    m = mm(past.astype(bf16), tail_ref[...])
    mr, mi = m[:, :TAPS], m[:, TAPS:]
    even = even_ref[...]
    spectrum = jnp.concatenate(
        [even * hr - (xr * mr + xi * mi), even * hi - (xr * mi - xi * mr)], axis=1)
    grad = fine_mm(spectrum, i_ref[...]) - base_ref[...]
    rows = jnp.concatenate(two(grad), axis=1)
    first = jnp.concatenate([line_ref[:16, :]] * (chunk // 16), axis=0)
    second = jnp.concatenate([line_ref[16:, :]] * (chunk // 16), axis=0)
    saves = []
    for k in range(chunks):
        at = lax.broadcasted_iota(jnp.int16, (chunk, ROWS), 0) + jnp.int16(k * chunk)
        both = mm(one_hot16(at, first, second), rows)
        out_ref[k * chunk:(k + 1) * chunk, :] = both[:, :TAPS] + both[:, TAPS:]
        saves.append(pltpu.make_async_copy(out_ref.at[parts[k]], out_hbm.at[parts[k]],
                                           sems.at[12 + chunks + k]))
        saves[-1].start()
    mine = as_bf16(iota((8, ROWS), 0) == srcloc_ref[...])
    both = mm(mine, rows)
    src_out_ref[...] = scale_src_ref[8:8 + SRC, :] - ((both[:, :TAPS] + both[:, TAPS:])
                                                      * scale_src_ref[:8, :])[:SRC]
    for save in saves:
        save.wait()


def settle_kernel(grads_ref, pick_ref, energy_ref, rcv_ref, cmp_ref, rcv_out_ref, cmp_out_ref):
    total = jnp.zeros((RCV + CMP, 2 * TAPS), f32)
    width = 512
    for k in range(SLOTS // width):
        rows = jnp.concatenate(two(grads_ref[k * width:(k + 1) * width, :]), axis=1)
        total = total + mm(pick_ref[:, k * width:(k + 1) * width], rows)
    change = (total[:, :TAPS] + total[:, TAPS:]) * energy_ref[...]
    rcv_out_ref[...] = rcv_ref[...] - change[:RCV]
    cmp_out_ref[...] = cmp_ref[...] - change[RCV:]


def shape(*dims, dtype=f32):
    return jax.ShapeDtypeStruct(dims, dtype)


VM = pl.BlockSpec(memory_space=pltpu.VMEM)
SM = pl.BlockSpec(memory_space=pltpu.SMEM)
HB = pl.BlockSpec(memory_space=pltpu.HBM)
DMA = pltpu.SemaphoreType.DMA
small = pltpu.CompilerParams(vmem_limit_bytes=24 * MIB)
large = pltpu.CompilerParams(vmem_limit_bytes=60 * MIB + MIB // 2)


def whole(array):
    return pl.BlockSpec(array.shape, lambda i: (0,) * len(array.shape))


def body(traces, targets, src_local, rcv_term, cmp_term, rcv_home, cmp_home, counts,
         src_filters, rcv_filters, cmp_filters):
    tables = {name: jnp.asarray(value) for name, value in make_tables().items()}
    src_line = src_local.reshape(1, ROWS)
    pay, slot_lines = pl.pallas_call(
        plan_kernel,
        out_shape=(shape(DEVS, 2 * PAIR), shape(8, ROWS)),
        in_specs=[SM, HB, HB, HB, HB, HB],
        out_specs=(VM, HB),
        scratch_shapes=[pltpu.VMEM((1, ROWS), i32), pltpu.VMEM((1, ROWS), i32),
                        pltpu.VMEM((128, 128), i32), pltpu.VMEM((256, 128), i32),
                        pltpu.VMEM((ROWS, NS), bf16), pltpu.VMEM((8, ROWS), f32), DMA((9,))],
        compiler_params=large,
        name="plan",
    )(counts, rcv_term.reshape(1, ROWS), cmp_term.reshape(1, ROWS),
      rcv_home.reshape(-1, 128), cmp_home.reshape(-1, 128), traces)
    got = lax.all_to_all(pay, AXES, split_axis=0, concat_axis=0, tiled=True)
    values = pl.pallas_call(
        pick_kernel,
        out_shape=shape(SLOTS, TAPS),
        in_specs=[VM] * 3, out_specs=HB,
        scratch_shapes=[pltpu.VMEM((SLOTS, TAPS), f32), DMA],
        compiler_params=small,
        name="pick",
    )(got, rcv_filters, cmp_filters)
    fetched = lax.all_to_all(values.reshape(DEVS, PAIR, TAPS), AXES, split_axis=0, concat_axis=0,
                             tiled=True).reshape(SLOTS, TAPS)

    def blk(width):
        return pl.BlockSpec((ROWBLK, width), lambda i: (i, 0))

    even, base, last = pl.pallas_call(
        lags_kernel,
        grid=(ROWS // ROWBLK,),
        out_shape=(shape(ROWS, TAPS), shape(ROWS, TAPS), shape(ROWS, WIN)),
        in_specs=[SM, pl.BlockSpec((8, 2 * PAIR), lambda i: (0, 0)), blk(NS), blk(NS)]
        + [whole(tables[n]) for n in "feicd"],
        out_specs=(blk(TAPS), blk(TAPS), blk(WIN)),
        compiler_params=large,
        cost_estimate=pl.CostEstimate(flops=5 * 10 ** 9, bytes_accessed=5 * 10 ** 6,
                                      transcendentals=0),
        name="lags",
    )(counts, got, traces, targets, *[tables[n] for n in "feicd"])
    int16 = jnp.int16
    book_shapes = (shape(RCV + CMP, SLOTS, dtype=bf16), shape(RCV + CMP, TAPS),
                   shape(ROWS, TAPS, dtype=int16), shape(ROWS, TAPS, dtype=int16),
                   shape(32, ROWS, dtype=int16), shape(ROWS, TAPS), shape(16, TAPS))
    book_in = (got, slot_lines, src_line, src_filters)
    settle_pick, energy, rcol, ccol, lines, shots, scale = pl.pallas_call(
        books_kernel,
        grid=(1,),
        out_shape=book_shapes,
        in_specs=[whole(a) for a in book_in], out_specs=[whole(a) for a in book_shapes],
        compiler_params=large,
        name="books",
    )(*book_in)
    held = (rcol, ccol, fetched, shots, tables["d"], last, tables["tail"], even, tables["i"], base,
            lines, src_line, scale)
    send, src_out = pl.pallas_call(
        grad_kernel,
        out_shape=(shape(SLOTS, TAPS), shape(SRC, TAPS)),
        in_specs=[HB] * len(held), out_specs=(HB, VM),
        scratch_shapes=[pltpu.VMEM(a.shape, a.dtype) for a in held]
        + [pltpu.VMEM((SLOTS, TAPS), f32), DMA((28,))],
        compiler_params=large,
        name="grad",
    )(*held)
    back = lax.all_to_all(send.reshape(DEVS, PAIR, TAPS), AXES, split_axis=0, concat_axis=0,
                          tiled=True).reshape(SLOTS, TAPS)
    rcv_out, cmp_out = pl.pallas_call(
        settle_kernel,
        out_shape=(shape(RCV, TAPS), shape(CMP, TAPS)),
        in_specs=[VM] * 5, out_specs=(VM, VM),
        compiler_params=small,
        name="settle",
    )(back, settle_pick, energy, rcv_filters, cmp_filters)
    return src_out, rcv_out, cmp_out


def solution(mesh):
    rows = P(AXES, None)
    flat = P(AXES)
    return jax.shard_map(
        body,
        mesh=mesh,
        in_specs=(rows, rows, flat, flat, flat, P(), P(), flat, rows, rows, rows),
        out_specs=(rows, rows, rows),
        check_vma=False,
    )
```

```python
import jax
import jax.numpy as jnp
import numpy as np
import ml_dtypes
from jax import lax
from jax.experimental import pallas as pl
from jax.experimental.pallas import tpu as pltpu
from jax.sharding import PartitionSpec as P

AXES = ("shot", "line")
DEVS = 128
ROWS = 512
NS = 2048
TAPS = 128
CAP = 8
PAIR = 2 * CAP
SLOTS = DEVS * PAIR
RCV = 128
CMP = 256
SRC = 4
WIN = 256
BLOCKS = NS // TAPS
ROWBLK = 128
step_size = 0.5
f32, bf16, i32 = jnp.float32, jnp.bfloat16, jnp.int32
NT = (((1,), (1,)), ((), ()))
MIB = 1024 * 1024


def split_pair(matrix):
    high = matrix.astype(ml_dtypes.bfloat16)
    low = (matrix - high.astype(np.float64)).astype(ml_dtypes.bfloat16)
    return high, low


def make_tables():
    angle = 2.0 * np.pi * (np.arange(TAPS) + 0.5) / WIN
    place = np.arange(WIN)
    phase = place[:, None] * angle[None, :]
    forward = np.concatenate([np.cos(phase), -np.sin(phase)], axis=1)
    inverse = forward.T / TAPS
    lag_phase = np.arange(TAPS)[:, None] * angle[None, :]
    even = 2.0 * np.cos(lag_phase)
    even[0] = 1.0
    f_high, f_low = split_pair(forward)
    d_pair = np.concatenate(split_pair(forward[:TAPS]), axis=0)
    e_pair = np.concatenate(split_pair(forward[TAPS:]), axis=0)
    i_pair = np.concatenate(split_pair(inverse[:, :TAPS]), axis=1)
    c_pair = np.concatenate(split_pair(even), axis=1)
    tail = split_pair(inverse[:, TAPS:] @ forward[TAPS:])[0]
    f_pair = np.concatenate([f_high, f_low], axis=0)
    return dict(f=f_pair, d=d_pair, e=e_pair, i=i_pair, c=c_pair, tail=tail)


def two(values):
    high = values.astype(bf16)
    low = (values - high.astype(f32)).astype(bf16)
    return high, low


def mm(a, b):
    return jnp.dot(a, b, preferred_element_type=f32)


def iota(shape, dim):
    return lax.broadcasted_iota(i32, shape, dim)


def as_bf16(mask):
    return mask.astype(f32).astype(bf16)


def fine_mm(values, pair):
    width = pair.shape[1] // 2
    high, low = two(values)
    both = mm(high, pair)
    return both[:, :width] + (both[:, width:] + mm(low, pair[:, :width]))


def fetch(hbm_refs, vmem_refs, sems):
    copies = [pltpu.make_async_copy(src, dst, sems.at[j])
              for j, (src, dst) in enumerate(zip(hbm_refs, vmem_refs))]
    for copy in copies:
        copy.start()
    return copies


def flag16(mask):
    return jnp.where(mask, jnp.ones(mask.shape, bf16), jnp.zeros(mask.shape, bf16))


def iota16(shape, dim):
    return lax.broadcasted_iota(jnp.int16, shape, dim)


def row16(row, count):
    tile = jnp.broadcast_to(row.astype(i32), (16, row.shape[1])).astype(jnp.int16)
    return jnp.concatenate([tile] * (count // 16), axis=0)


def plan_kernel(count_ref, rterm_hbm, cterm_hbm, rhome_hbm, chome_hbm, traces_hbm, pay_ref, slot_ref,
                rterm_ref, cterm_ref, rhome_ref, chome_ref, tbuf, sems):
    parts = [pl.ds(j * 128, 128) for j in range(4)]
    copies = fetch(
        [rterm_hbm, cterm_hbm, rhome_hbm, chome_hbm] + [traces_hbm.at[p] for p in parts],
        [rterm_ref, cterm_ref, rhome_ref, chome_ref] + [tbuf.at[p] for p in parts], sems)
    earlier = flag16(iota16((128, 128), 0) < iota16((128, 128), 1))
    count_up = jnp.concatenate([earlier, jnp.ones((128, 128), bf16)], axis=1)

    def look_up(term, home, bits):
        high, low = term >> 7, term & 127
        halves = jnp.concatenate([jnp.transpose((home >> bits).astype(f32)),
                                  jnp.transpose((home & (2 ** bits - 1)).astype(f32))], axis=0)
        rows = home.shape[0]
        both = mm(halves.astype(bf16), flag16(iota16((rows, ROWS), 0) == row16(high, rows)))
        pick_low = iota((128, ROWS), 0) == low
        return (jnp.sum(jnp.where(pick_low, both[:128], 0.0), axis=0, keepdims=True),
                jnp.sum(jnp.where(pick_low, both[128:], 0.0), axis=0, keepdims=True))

    for copy in copies[:4]:
        copy.wait()
    r_owner, r_place = look_up(rterm_ref[...], rhome_ref[...], 7)
    c_owner, c_place = look_up(cterm_ref[...], chome_ref[...], 8)
    for copy in copies[4:]:
        copy.wait()
    line128 = iota16((DEVS, ROWS), 0)
    mine16 = [flag16(line128 == row16(owner, DEVS)) for owner in (r_owner, c_owner)]
    mine = jnp.concatenate(mine16, axis=0)
    owners = jnp.concatenate(
        [jnp.broadcast_to(r_owner, (DEVS, ROWS)), jnp.broadcast_to(c_owner, (DEVS, ROWS))], axis=0)
    here = owners == (iota((2 * DEVS, ROWS), 0) & (DEVS - 1)).astype(f32)
    past = jnp.zeros((2 * DEVS, 128), f32)
    ranks, powers = [], []
    for j in range(4):
        part = slice(j * 128, (j + 1) * 128)
        seen = mm(mine[:, part], count_up)
        before = jnp.where(here[:, part], seen[:, :128] + past, 0.0)
        past = past + seen[:, 128:]
        ranks.append(jnp.concatenate([jnp.sum(before[:DEVS], axis=0, keepdims=True),
                                      jnp.sum(before[DEVS:], axis=0, keepdims=True)], axis=0))
        total = jnp.zeros((128, 128), f32)
        for b in range(BLOCKS):
            x = tbuf[part, b * 128:(b + 1) * 128].astype(f32)
            total = total + x * x
        powers.append(jnp.sum(jnp.transpose(total), axis=0, keepdims=True))
    rank = jnp.concatenate(ranks, axis=1)
    r_rank, c_rank = rank[0:1], rank[1:2] + CAP
    live = (iota((1, ROWS), 1) < count_ref[0]).astype(f32)
    power = jnp.concatenate(powers, axis=1) * live
    slot_ref[...] = jnp.concatenate(
        [r_owner * PAIR + r_rank, c_owner * PAIR + c_rank, live, power, jnp.zeros((4, ROWS), f32)],
        axis=0)
    p_high = power.astype(bf16).astype(f32)
    p_low = power - p_high
    line = iota((PAIR, ROWS), 0).astype(f32)

    def weights(rank, place):
        at = line == rank
        return jnp.concatenate(
            [jnp.where(at, row, 0.0) for row in (place, p_high, p_low)], axis=0).astype(bf16)

    pay_ref[...] = lax.dot_general(
        jnp.concatenate(mine16, axis=1),
        jnp.concatenate([weights(r_rank, r_place), weights(c_rank, c_place)], axis=1),
        NT, preferred_element_type=f32)


def pick_kernel(got_ref, rcv_ref, cmp_ref, out_hbm, out_ref, sems):
    pairs = [jnp.concatenate(two(t[...]), axis=1) for t in (rcv_ref, cmp_ref)]
    half = DEVS // 2
    saves = []
    for h in range(2):
        got = got_ref[h * half:(h + 1) * half, :PAIR].astype(i32)
        for side, pair in enumerate(pairs):
            lane = iota((half, pair.shape[0]), 1)
            pick = jnp.concatenate(
                [as_bf16(lane == got[:, s:s + 1]) for s in range(side * CAP, (side + 1) * CAP)], axis=0)
            both = mm(pick, pair)
            values = both[:, :TAPS] + both[:, TAPS:]
            for s in range(CAP):
                out_ref[pl.ds(h * half * PAIR + side * CAP + s, half, stride=PAIR), :] = (
                    values[s * half:(s + 1) * half])
        part = pl.ds(h * half * PAIR, half * PAIR)
        saves.append(pltpu.make_async_copy(out_ref.at[part], out_hbm.at[part], sems.at[h]))
        saves[-1].start()
    for save in saves:
        save.wait()


def lags_kernel(after_ref, traces_ref, targets_ref, f_ref, e_ref, i_ref, c_ref, d_ref,
                even_ref, base_ref, last_ref):
    f_high, f_low = f_ref[:WIN, :], f_ref[WIN:, :]
    e_pair = e_ref[...]
    own = jnp.zeros((ROWBLK, WIN), f32)
    cross = jnp.zeros((ROWBLK, WIN), f32)
    for b in range(BLOCKS):
        now = traces_ref[:, b * 128:(b + 1) * 128]
        goal = targets_ref[:, b * 128:(b + 1) * 128]
        u = mm(jnp.concatenate([now, now], axis=1), e_pair)
        v = mm(jnp.concatenate([goal, goal], axis=1), e_pair)
        if b == 0:
            x = u
        else:
            window = traces_ref[:, (b - 1) * 128:(b + 1) * 128]
            x = mm(window, f_high) + mm(window, f_low)
        xr, xi = x[:, :TAPS], x[:, TAPS:]
        ur, ui = u[:, :TAPS], u[:, TAPS:]
        vr, vi = v[:, :TAPS], v[:, TAPS:]
        own = own + jnp.concatenate([xr * ur + xi * ui, xr * ui - xi * ur], axis=1)
        cross = cross + jnp.concatenate([xr * vr + xi * vi, xr * vi - xi * vr], axis=1)
    i_pair = i_ref[...]
    even_ref[...] = fine_mm(fine_mm(own, i_pair), c_ref[...])
    base_ref[...] = fine_mm(cross, i_pair)
    final = traces_ref[:, (BLOCKS - 1) * 128:]
    last_ref[...] = mm(jnp.concatenate([final, final], axis=1), d_ref[...])


def books_kernel(got_ref, slot_ref, srcloc_ref, src_ref,
                 settle_ref, energy_ref, rcol_ref, ccol_ref, line_ref, shot_ref, scale_ref):
    got = jnp.concatenate([got_ref[...], jnp.zeros((DEVS, 128 - 3 * PAIR), f32)], axis=1)
    turned = jnp.transpose(got)[:3 * PAIR].astype(bf16)
    q = iota((DEVS, SLOTS), 1)
    spread = as_bf16((q >> 4) == iota((DEVS, SLOTS), 0))
    wide = mm(turned, spread)
    line = iota((PAIR, SLOTS), 0)
    slot = iota((PAIR, SLOTS), 1) & (PAIR - 1)
    place = jnp.sum(jnp.where(line == slot, wide[:PAIR], 0.0), axis=0, keepdims=True)
    power = jnp.sum(jnp.where(line == slot, wide[PAIR:2 * PAIR] + wide[2 * PAIR:], 0.0), axis=0, keepdims=True)
    place = place.astype(i32) + ((iota((1, SLOTS), 1) & CAP) << 4)
    for c in range(3):
        rows = iota((128, SLOTS), 0) + c * 128
        settle_ref[c * 128:(c + 1) * 128, :] = as_bf16(rows == place)
        energy = jnp.sum(jnp.where(rows == place, power, 0.0), axis=1, keepdims=True)
        energy_ref[c * 128:(c + 1) * 128, :] = jnp.broadcast_to(
            step_size / jnp.maximum(energy, 1.0), (128, 128))
    lines = jnp.concatenate(
        [slot_ref[...], srcloc_ref[...].astype(f32), jnp.zeros((128 - 9, ROWS), f32)], axis=0)
    src = src_ref[...]
    for j in range(4):
        part = slice(j * 128, (j + 1) * 128)
        col = jnp.transpose(lines[:, part])
        rcol_ref[part, :] = jnp.broadcast_to(col[:, 0:1].astype(i32), (128, 128)).astype(jnp.int16)
        ccol_ref[part, :] = jnp.broadcast_to(col[:, 1:2].astype(i32), (128, 128)).astype(jnp.int16)
        src_rows = jnp.zeros((128, TAPS), f32)
        for s in range(SRC):
            src_rows = jnp.where(col[:, 8:9] == float(s), src[s:s + 1, :], src_rows)
        shot_ref[part, :] = src_rows
    live = slot_ref[2:3, :] > 0.0
    for j, row in enumerate((slot_ref[0:1, :], slot_ref[1:2, :], srcloc_ref[...].astype(f32))):
        line_ref[16 * j:16 * (j + 1), :] = jnp.broadcast_to(
            jnp.where(live, row, -1.0).astype(i32), (16, ROWS)).astype(jnp.int16)
    mine = iota((8, ROWS), 0) == srcloc_ref[...]
    energy = jnp.sum(jnp.where(mine, slot_ref[3:4, :], 0.0), axis=1, keepdims=True)
    scale_ref[:8, :] = jnp.broadcast_to(step_size / jnp.maximum(energy, 1.0), (8, TAPS))
    scale_ref[8:, :] = jnp.concatenate([src, jnp.zeros((8 - SRC, TAPS), f32)], axis=0)


def one_hot16(at, first, second):
    ones = jnp.ones(at.shape, bf16)
    return jnp.where((at == first) | (at == second), ones, jnp.zeros(at.shape, bf16))


def grad_kernel(fetched_ref, *refs):
    hbm_refs, (out_ref, src_out_ref) = refs[:11], refs[11:13]
    vmem_refs, sems = refs[13:24], refs[24]
    copies = fetch(hbm_refs, vmem_refs, sems)
    (rcol_ref, ccol_ref, shot_ref, d_ref, even_ref, last_ref, tail_ref, i_ref, base_ref,
     line_ref, scale_ref) = vmem_refs
    chunk = 512
    chunks = SLOTS // chunk
    lane = iota16((ROWS, 128), 1)
    first_rows = jnp.concatenate(two(fetched_ref[:chunk, :]), axis=1)
    for copy in copies[:2]:
        copy.wait()
    rcol, ccol = rcol_ref[...], ccol_ref[...]
    both = None
    for k in range(chunks):
        pick = jnp.concatenate(
            [one_hot16(lane + jnp.int16(k * chunk + j * 128), rcol, ccol) for j in range(chunk // 128)],
            axis=1)
        if k == 0:
            both = mm(pick, first_rows)
        else:
            rows = jnp.concatenate(two(fetched_ref[k * chunk:(k + 1) * chunk, :]), axis=1)
            both = both + mm(pick, rows)
    for copy in copies[2:]:
        copy.wait()
    mixed = (shot_ref[...] + (both[:, :TAPS] + both[:, TAPS:])).astype(bf16)
    h = mm(jnp.concatenate([mixed, mixed], axis=1), d_ref[...])
    hr, hi = h[:, :TAPS], h[:, TAPS:]
    xr, xi = last_ref[:, :TAPS], last_ref[:, TAPS:]
    past = jnp.concatenate([xr * hr - xi * hi, xr * hi + xi * hr], axis=1)
    m = mm(past.astype(bf16), tail_ref[...])
    mr, mi = m[:, :TAPS], m[:, TAPS:]
    even = even_ref[...]
    spectrum = jnp.concatenate(
        [even * hr - (xr * mr + xi * mi), even * hi - (xr * mi - xi * mr)], axis=1)
    grad = fine_mm(spectrum, i_ref[...]) - base_ref[...]
    rows = jnp.concatenate(two(grad), axis=1)
    first = jnp.concatenate([line_ref[:16, :]] * (chunk // 16), axis=0)
    second = jnp.concatenate([line_ref[16:32, :]] * (chunk // 16), axis=0)
    for k in range(chunks):
        at = iota16((chunk, ROWS), 0) + jnp.int16(k * chunk)
        both = mm(one_hot16(at, first, second), rows)
        out_ref[k * chunk:(k + 1) * chunk, :] = both[:, :TAPS] + both[:, TAPS:]
    both = mm(flag16(iota16((16, ROWS), 0) == line_ref[32:, :]), rows)
    src_out_ref[...] = scale_ref[8:8 + SRC, :] - ((both[:8, :TAPS] + both[:8, TAPS:])
                                                  * scale_ref[:8, :])[:SRC]


def settle_kernel(grads_ref, pick_ref, energy_ref, rcv_ref, cmp_ref, rcv_out_ref, cmp_out_ref):
    total = jnp.zeros((RCV + CMP, 2 * TAPS), f32)
    width = 512
    for k in range(SLOTS // width):
        rows = jnp.concatenate(two(grads_ref[k * width:(k + 1) * width, :]), axis=1)
        total = total + mm(pick_ref[:, k * width:(k + 1) * width], rows)
    change = (total[:, :TAPS] + total[:, TAPS:]) * energy_ref[...]
    rcv_out_ref[...] = rcv_ref[...] - change[:RCV]
    cmp_out_ref[...] = cmp_ref[...] - change[RCV:]


def shape(*dims, dtype=f32):
    return jax.ShapeDtypeStruct(dims, dtype)


VM = pl.BlockSpec(memory_space=pltpu.VMEM)
HB = pl.BlockSpec(memory_space=pltpu.HBM)
DMA = pltpu.SemaphoreType.DMA
small = pltpu.CompilerParams(vmem_limit_bytes=24 * MIB)
large = pltpu.CompilerParams(vmem_limit_bytes=60 * MIB + MIB // 2)


def whole(array):
    return pl.BlockSpec(array.shape, lambda i: (0,) * len(array.shape))


def in_hbm(*arrays):
    return [pltpu.with_memory_space_constraint(a, pltpu.HBM) for a in arrays]


def hbm(*dims, dtype=f32):
    return pltpu.HBM(dims, dtype)


def vmem(*dims, dtype=f32):
    return pltpu.VMEM(dims, dtype)


def run_plan(traces, rcv_term, cmp_term, rcv_home, cmp_home, counts):
    args = in_hbm(rcv_term.reshape(1, ROWS), cmp_term.reshape(1, ROWS),
                  rcv_home.reshape(-1, 128), cmp_home.reshape(-1, 128), traces)
    return pl.pallas_call(
        plan_kernel,
        out_shape=(vmem(DEVS, 3 * PAIR), vmem(8, ROWS)),
        in_specs=[pl.BlockSpec(memory_space=pltpu.SMEM)] + [HB] * 5,
        out_specs=(VM, VM),
        scratch_shapes=[vmem(1, ROWS, dtype=i32), vmem(1, ROWS, dtype=i32),
                        vmem(128, 128, dtype=i32), vmem(256, 128, dtype=i32),
                        vmem(ROWS, NS, dtype=bf16), DMA((8,))],
        compiler_params=small,
        name="plan",
    )(counts, *args)


def run_pick(got, rcv_filters, cmp_filters):
    return pl.pallas_call(
        pick_kernel,
        out_shape=hbm(SLOTS, TAPS),
        in_specs=[VM] * 3, out_specs=HB,
        scratch_shapes=[vmem(SLOTS, TAPS), DMA((2,))],
        compiler_params=small,
        name="pick",
    )(got, rcv_filters, cmp_filters)


def run_lags(got, traces, targets, tables):
    def blk(width):
        return pl.BlockSpec((ROWBLK, width), lambda i: (i, 0))

    return pl.pallas_call(
        lags_kernel,
        grid=(ROWS // ROWBLK,),
        out_shape=(hbm(ROWS, TAPS), hbm(ROWS, TAPS), hbm(ROWS, WIN)),
        in_specs=[pl.BlockSpec((8, 3 * PAIR), lambda i: (0, 0)), blk(NS), blk(NS)]
        + [whole(tables[n]) for n in "feicd"],
        out_specs=(blk(TAPS), blk(TAPS), blk(WIN)),
        compiler_params=large,
        cost_estimate=pl.CostEstimate(flops=5 * 10 ** 9, bytes_accessed=5 * 10 ** 6,
                                      transcendentals=0),
        name="lags",
    )(*in_hbm(got, traces, targets, *[tables[n] for n in "feicd"]))


def run_books(got, slot_lines, src_line, src_filters):
    int16 = jnp.int16
    out = (hbm(RCV + CMP, SLOTS, dtype=bf16), hbm(RCV + CMP, TAPS),
           hbm(ROWS, TAPS, dtype=int16), hbm(ROWS, TAPS, dtype=int16),
           hbm(48, ROWS, dtype=int16), hbm(ROWS, TAPS), hbm(16, TAPS))
    args = (got, slot_lines, src_line, src_filters)
    return pl.pallas_call(
        books_kernel,
        grid=(1,),
        out_shape=out,
        in_specs=[whole(a) for a in args], out_specs=[whole(a) for a in out],
        compiler_params=large,
        name="books",
    )(got, slot_lines, *in_hbm(*args[2:]))


def run_grad(fetched, held):
    return pl.pallas_call(
        grad_kernel,
        out_shape=(vmem(SLOTS, TAPS), vmem(SRC, TAPS)),
        in_specs=[VM] + [HB] * len(held), out_specs=(VM, VM),
        scratch_shapes=[vmem(*a.shape, dtype=a.dtype) for a in held] + [DMA((len(held),))],
        compiler_params=small,
        name="grad",
    )(pltpu.with_memory_space_constraint(fetched, pltpu.VMEM), *in_hbm(*held))


def run_settle(back, settle_pick, energy, rcv_filters, cmp_filters):
    return pl.pallas_call(
        settle_kernel,
        out_shape=(shape(RCV, TAPS), shape(CMP, TAPS)),
        in_specs=[VM] * 5, out_specs=(VM, VM),
        compiler_params=small,
        name="settle",
    )(back, settle_pick, energy, rcv_filters, cmp_filters)


def swap(rows):
    return lax.all_to_all(rows.reshape(DEVS, PAIR, TAPS), AXES, split_axis=0, concat_axis=0,
                          tiled=True).reshape(SLOTS, TAPS)


def body(traces, targets, src_local, rcv_term, cmp_term, rcv_home, cmp_home, counts,
         src_filters, rcv_filters, cmp_filters):
    tables = {name: jnp.asarray(value) for name, value in make_tables().items()}
    src_line = src_local.reshape(1, ROWS)
    pay, slot_lines = run_plan(traces, rcv_term, cmp_term, rcv_home, cmp_home, counts)
    got = lax.all_to_all(pay, AXES, split_axis=0, concat_axis=0, tiled=True)
    fetched = swap(run_pick(got, rcv_filters, cmp_filters))
    even, base, last = run_lags(got, traces, targets, tables)
    settle_pick, energy, rcol, ccol, lines, shots, scale = run_books(
        got, slot_lines, src_line, src_filters)
    send, src_out = run_grad(fetched, (rcol, ccol, shots, tables["d"], even, last, tables["tail"],
                                       tables["i"], base, lines, scale))
    rcv_out, cmp_out = run_settle(swap(send), settle_pick, energy, rcv_filters, cmp_filters)
    return src_out, rcv_out, cmp_out


def solution(mesh):
    rows = P(AXES, None)
    flat = P(AXES)
    return jax.shard_map(
        body,
        mesh=mesh,
        in_specs=(rows, rows, flat, flat, flat, P(), P(), flat, rows, rows, rows),
        out_specs=(rows, rows, rows),
        check_vma=False,
    )
```

```python
import jax
import jax.numpy as jnp
import numpy as np
import ml_dtypes
from jax import lax
from jax.experimental import pallas as pl
from jax.experimental.pallas import tpu as pltpu
from jax.sharding import PartitionSpec as P

AXES = ("shot", "line")
DEVS = 128
ROWS = 512
NS = 2048
TAPS = 128
CAP = 8
PAIR = 2 * CAP
SLOTS = DEVS * PAIR
RCV = 128
CMP = 256
SRC = 4
WIN = 256
BLOCKS = NS // TAPS
ROWBLK = 256
step_size = 0.5
f32, bf16, i32 = jnp.float32, jnp.bfloat16, jnp.int32
NT = (((1,), (1,)), ((), ()))
MIB = 1024 * 1024


def split_pair(matrix):
    high = matrix.astype(ml_dtypes.bfloat16)
    low = (matrix - high.astype(np.float64)).astype(ml_dtypes.bfloat16)
    return high, low


def make_tables():
    angle = 2.0 * np.pi * (np.arange(TAPS) + 0.5) / WIN
    place = np.arange(WIN)
    phase = place[:, None] * angle[None, :]
    forward = np.concatenate([np.cos(phase), -np.sin(phase)], axis=1)
    inverse = forward.T / TAPS
    lag_phase = np.arange(TAPS)[:, None] * angle[None, :]
    even = 2.0 * np.cos(lag_phase)
    even[0] = 1.0
    d_pair = np.concatenate(split_pair(forward[:TAPS]), axis=0)
    e_pair = np.concatenate(split_pair(forward[TAPS:]), axis=0)
    i_pair = np.concatenate(split_pair(inverse[:, :TAPS]), axis=1)
    c_pair = np.concatenate(split_pair(even), axis=1)
    tail = split_pair(inverse[:, TAPS:] @ forward[TAPS:])[0]
    return dict(d=d_pair, e=e_pair, i=i_pair, c=c_pair, tail=tail)


def two(values):
    high = values.astype(bf16)
    low = (values - high.astype(f32)).astype(bf16)
    return high, low


def mm(a, b):
    return jnp.dot(a, b, preferred_element_type=f32)


def iota(shape, dim):
    return lax.broadcasted_iota(i32, shape, dim)


def as_bf16(mask):
    return mask.astype(f32).astype(bf16)


def fine_mm(values, pair):
    width = pair.shape[1] // 2
    high, low = two(values)
    both = mm(high, pair)
    return both[:, :width] + (both[:, width:] + mm(low, pair[:, :width]))


def fetch(hbm_refs, vmem_refs, sems):
    copies = [pltpu.make_async_copy(src, dst, sems.at[j])
              for j, (src, dst) in enumerate(zip(hbm_refs, vmem_refs))]
    for copy in copies:
        copy.start()
    return copies


def flag16(mask):
    return jnp.where(mask, jnp.ones(mask.shape, bf16), jnp.zeros(mask.shape, bf16))


def iota16(shape, dim):
    return lax.broadcasted_iota(jnp.int16, shape, dim)


def row16(row, count):
    tile = jnp.broadcast_to(row.astype(i32), (16, row.shape[1])).astype(jnp.int16)
    return jnp.concatenate([tile] * (count // 16), axis=0)


def plan_kernel(count_ref, rterm_hbm, cterm_hbm, rhome_hbm, chome_hbm, traces_hbm, pay_ref, slot_ref,
                rterm_ref, cterm_ref, rhome_ref, chome_ref, tbuf, sems):
    parts = [pl.ds(j * 128, 128) for j in range(4)]
    copies = fetch(
        [rterm_hbm, cterm_hbm, rhome_hbm, chome_hbm] + [traces_hbm.at[p] for p in parts],
        [rterm_ref, cterm_ref, rhome_ref, chome_ref] + [tbuf.at[p] for p in parts], sems)
    earlier = flag16(iota16((128, 128), 0) < iota16((128, 128), 1))
    count_up = jnp.concatenate([earlier, jnp.ones((128, 128), bf16)], axis=1)

    def look_up(term, home, bits):
        high, low = term >> 7, term & 127
        halves = jnp.concatenate([home >> bits, home & (2 ** bits - 1)], axis=0)
        rows = home.shape[0]
        both = mm(halves.astype(f32).astype(bf16), flag16(iota16((128, ROWS), 0) == row16(low, 128)))
        pick_high = iota((rows, ROWS), 0) == high
        return (jnp.sum(jnp.where(pick_high, both[:rows], 0.0), axis=0, keepdims=True),
                jnp.sum(jnp.where(pick_high, both[rows:], 0.0), axis=0, keepdims=True))

    for copy in copies[:4]:
        copy.wait()
    r_owner, r_place = look_up(rterm_ref[...], rhome_ref[...], 7)
    c_owner, c_place = look_up(cterm_ref[...], chome_ref[...], 8)
    for copy in copies[4:]:
        copy.wait()
    line128 = iota16((DEVS, ROWS), 0)
    mine16 = [flag16(line128 == row16(owner, DEVS)) for owner in (r_owner, c_owner)]
    mine = jnp.concatenate(mine16, axis=0)
    owners = jnp.concatenate(
        [jnp.broadcast_to(r_owner, (DEVS, ROWS)), jnp.broadcast_to(c_owner, (DEVS, ROWS))], axis=0)
    here = owners == (iota((2 * DEVS, ROWS), 0) & (DEVS - 1)).astype(f32)
    past = jnp.zeros((2 * DEVS, 128), f32)
    ranks, powers = [], []
    for j in range(4):
        part = slice(j * 128, (j + 1) * 128)
        seen = mm(mine[:, part], count_up)
        before = jnp.where(here[:, part], seen[:, :128] + past, 0.0)
        past = past + seen[:, 128:]
        ranks.append(jnp.concatenate([jnp.sum(before[:DEVS], axis=0, keepdims=True),
                                      jnp.sum(before[DEVS:], axis=0, keepdims=True)], axis=0))
        total = jnp.zeros((128, 128), f32)
        for b in range(BLOCKS):
            x = tbuf[part, b * 128:(b + 1) * 128].astype(f32)
            total = total + x * x
        powers.append(jnp.sum(jnp.transpose(total), axis=0, keepdims=True))
    rank = jnp.concatenate(ranks, axis=1)
    r_rank, c_rank = rank[0:1], rank[1:2] + CAP
    live = (iota((1, ROWS), 1) < count_ref[0]).astype(f32)
    power = jnp.concatenate(powers, axis=1) * live
    slot_ref[...] = jnp.concatenate(
        [r_owner * PAIR + r_rank, c_owner * PAIR + c_rank, live, power, jnp.zeros((4, ROWS), f32)],
        axis=0)
    p_high = power.astype(bf16).astype(f32)
    p_low = power - p_high
    line = iota((PAIR, ROWS), 0).astype(f32)

    def weights(rank, place):
        at = line == rank
        return jnp.concatenate(
            [jnp.where(at, row, 0.0) for row in (place, p_high, p_low)], axis=0).astype(bf16)

    pay_ref[...] = lax.dot_general(
        jnp.concatenate(mine16, axis=1),
        jnp.concatenate([weights(r_rank, r_place), weights(c_rank, c_place)], axis=1),
        NT, preferred_element_type=f32)


def pick_kernel(got_ref, rcv_ref, cmp_ref, out_hbm, out_ref, sems):
    pairs = [jnp.concatenate(two(t[...]), axis=1) for t in (rcv_ref, cmp_ref)]
    half = DEVS // 4
    saves = []
    for h in range(4):
        got = got_ref[h * half:(h + 1) * half, :PAIR].astype(i32)
        for side, pair in enumerate(pairs):
            lane = iota((half, pair.shape[0]), 1)
            pick = jnp.concatenate(
                [as_bf16(lane == got[:, s:s + 1]) for s in range(side * CAP, (side + 1) * CAP)], axis=0)
            both = mm(pick, pair)
            values = both[:, :TAPS] + both[:, TAPS:]
            for s in range(CAP):
                out_ref[pl.ds(h * half * PAIR + side * CAP + s, half, stride=PAIR), :] = (
                    values[s * half:(s + 1) * half])
        part = pl.ds(h * half * PAIR, half * PAIR)
        saves.append(pltpu.make_async_copy(out_ref.at[part], out_hbm.at[part], sems.at[h]))
        saves[-1].start()
    for save in saves:
        save.wait()


def lags_kernel(after_ref, traces_ref, targets_ref, e_ref, i_ref, c_ref,
                even_ref, base_ref, last_ref):
    e_pair = e_ref[...]
    sign = 1.0 - 2.0 * (iota((1, TAPS), 1) & 1).astype(f32)
    own = [jnp.zeros((ROWBLK, TAPS), f32)] * 2
    cross = [jnp.zeros((ROWBLK, TAPS), f32)] * 2
    back = None
    for b in range(BLOCKS):
        now = traces_ref[:, b * 128:(b + 1) * 128]
        goal = targets_ref[:, b * 128:(b + 1) * 128]
        u = mm(jnp.concatenate([now, now], axis=1), e_pair)
        v = mm(jnp.concatenate([goal, goal], axis=1), e_pair)
        ur, ui = u[:, :TAPS], u[:, TAPS:]
        vr, vi = v[:, :TAPS], v[:, TAPS:]
        xr, xi = (ur, ui) if b == 0 else (ur + back[0], ui + back[1])
        own = [own[0] + (xr * ur + xi * ui), own[1] + (xr * ui - xi * ur)]
        cross = [cross[0] + (xr * vr + xi * vi), cross[1] + (xr * vi - xi * vr)]
        back = -sign * ui, sign * ur
    i_pair = i_ref[...]
    even_ref[...] = fine_mm(fine_mm(jnp.concatenate(own, axis=1), i_pair), c_ref[...])
    base_ref[...] = fine_mm(jnp.concatenate(cross, axis=1), i_pair)
    last_ref[...] = jnp.concatenate(back, axis=1)


def books_kernel(got_ref, slot_ref, srcloc_ref, src_ref,
                 settle_ref, energy_ref, rcol_ref, ccol_ref, line_ref, shot_ref, scale_ref):
    got = jnp.concatenate([got_ref[...], jnp.zeros((DEVS, 128 - 3 * PAIR), f32)], axis=1)
    turned = jnp.transpose(got)[:3 * PAIR].astype(bf16)
    q = iota((DEVS, SLOTS), 1)
    spread = as_bf16((q >> 4) == iota((DEVS, SLOTS), 0))
    wide = mm(turned, spread)
    line = iota((PAIR, SLOTS), 0)
    slot = iota((PAIR, SLOTS), 1) & (PAIR - 1)
    place = jnp.sum(jnp.where(line == slot, wide[:PAIR], 0.0), axis=0, keepdims=True)
    power = jnp.sum(jnp.where(line == slot, wide[PAIR:2 * PAIR] + wide[2 * PAIR:], 0.0), axis=0, keepdims=True)
    place = place.astype(i32) + ((iota((1, SLOTS), 1) & CAP) << 4)
    for c in range(3):
        rows = iota((128, SLOTS), 0) + c * 128
        settle_ref[c * 128:(c + 1) * 128, :] = as_bf16(rows == place)
        energy = jnp.sum(jnp.where(rows == place, power, 0.0), axis=1, keepdims=True)
        energy_ref[c * 128:(c + 1) * 128, :] = jnp.broadcast_to(
            step_size / jnp.maximum(energy, 1.0), (128, 128))
    lines = jnp.concatenate(
        [slot_ref[...], srcloc_ref[...].astype(f32), jnp.zeros((128 - 9, ROWS), f32)], axis=0)
    src = src_ref[...]
    for j in range(4):
        part = slice(j * 128, (j + 1) * 128)
        col = jnp.transpose(lines[:, part])
        rcol_ref[part, :] = jnp.broadcast_to(col[:, 0:1].astype(i32), (128, 128)).astype(jnp.int16)
        ccol_ref[part, :] = jnp.broadcast_to(col[:, 1:2].astype(i32), (128, 128)).astype(jnp.int16)
        src_rows = jnp.zeros((128, TAPS), f32)
        for s in range(SRC):
            src_rows = jnp.where(col[:, 8:9] == float(s), src[s:s + 1, :], src_rows)
        shot_ref[part, :] = src_rows
    live = slot_ref[2:3, :] > 0.0
    for j, row in enumerate((slot_ref[0:1, :], slot_ref[1:2, :], srcloc_ref[...].astype(f32))):
        line_ref[16 * j:16 * (j + 1), :] = jnp.broadcast_to(
            jnp.where(live, row, -1.0).astype(i32), (16, ROWS)).astype(jnp.int16)
    mine = iota((8, ROWS), 0) == srcloc_ref[...]
    energy = jnp.sum(jnp.where(mine, slot_ref[3:4, :], 0.0), axis=1, keepdims=True)
    scale_ref[:8, :] = jnp.broadcast_to(step_size / jnp.maximum(energy, 1.0), (8, TAPS))
    scale_ref[8:, :] = jnp.concatenate([src, jnp.zeros((8 - SRC, TAPS), f32)], axis=0)


def one_hot16(at, first, second):
    ones = jnp.ones(at.shape, bf16)
    return jnp.where((at == first) | (at == second), ones, jnp.zeros(at.shape, bf16))


def grad_kernel(fetched_ref, *refs):
    hbm_refs, (out_ref, src_out_ref) = refs[:11], refs[11:13]
    vmem_refs, rows_ref, sems = refs[13:24], refs[24], refs[25]
    copies = fetch(hbm_refs, vmem_refs, sems)
    (rcol_ref, ccol_ref, shot_ref, d_ref, even_ref, last_ref, tail_ref, i_ref, base_ref,
     line_ref, scale_ref) = vmem_refs
    chunk = 512
    chunks = SLOTS // chunk
    lane = iota16((ROWS, 128), 1)
    for k in range(chunks):
        part = slice(k * chunk, (k + 1) * chunk)
        rows_ref[part, :] = jnp.concatenate(two(fetched_ref[part, :]), axis=1)
    for copy in copies[:2]:
        copy.wait()
    rcol, ccol = rcol_ref[...], ccol_ref[...]
    both = None
    for k in range(chunks):
        pick = jnp.concatenate(
            [one_hot16(lane + jnp.int16(k * chunk + j * 128), rcol, ccol) for j in range(chunk // 128)],
            axis=1)
        part = mm(pick, rows_ref[k * chunk:(k + 1) * chunk, :])
        both = part if k == 0 else both + part
    for copy in copies[2:]:
        copy.wait()
    mixed = (shot_ref[...] + (both[:, :TAPS] + both[:, TAPS:])).astype(bf16)
    h = mm(jnp.concatenate([mixed, mixed], axis=1), d_ref[...])
    hr, hi = h[:, :TAPS], h[:, TAPS:]
    xr, xi = last_ref[:, :TAPS], last_ref[:, TAPS:]
    past = jnp.concatenate([xr * hr - xi * hi, xr * hi + xi * hr], axis=1)
    m = mm(past.astype(bf16), tail_ref[...])
    mr, mi = m[:, :TAPS], m[:, TAPS:]
    even = even_ref[...]
    spectrum = jnp.concatenate(
        [even * hr - (xr * mr + xi * mi), even * hi - (xr * mi - xi * mr)], axis=1)
    grad = fine_mm(spectrum, i_ref[...]) - base_ref[...]
    rows = jnp.concatenate(two(grad), axis=1)
    first = jnp.concatenate([line_ref[:16, :]] * (chunk // 16), axis=0)
    second = jnp.concatenate([line_ref[16:32, :]] * (chunk // 16), axis=0)
    for k in range(chunks):
        at = iota16((chunk, ROWS), 0) + jnp.int16(k * chunk)
        both = mm(one_hot16(at, first, second), rows)
        out_ref[k * chunk:(k + 1) * chunk, :] = both[:, :TAPS] + both[:, TAPS:]
    both = mm(flag16(iota16((16, ROWS), 0) == line_ref[32:, :]), rows)
    src_out_ref[...] = scale_ref[8:8 + SRC, :] - ((both[:8, :TAPS] + both[:8, TAPS:])
                                                  * scale_ref[:8, :])[:SRC]


def settle_kernel(grads_ref, pick_ref, energy_ref, rcv_ref, cmp_ref, src_ref,
                  src_out_ref, rcv_out_ref, cmp_out_ref):
    src_out_ref[...] = src_ref[...]
    total = jnp.zeros((RCV + CMP, 2 * TAPS), f32)
    width = 512
    for k in range(SLOTS // width):
        rows = jnp.concatenate(two(grads_ref[k * width:(k + 1) * width, :]), axis=1)
        total = total + mm(pick_ref[:, k * width:(k + 1) * width], rows)
    change = (total[:, :TAPS] + total[:, TAPS:]) * energy_ref[...]
    rcv_out_ref[...] = rcv_ref[...] - change[:RCV]
    cmp_out_ref[...] = cmp_ref[...] - change[RCV:]


def shape(*dims, dtype=f32):
    return jax.ShapeDtypeStruct(dims, dtype)


VM = pl.BlockSpec(memory_space=pltpu.VMEM)
HB = pl.BlockSpec(memory_space=pltpu.HBM)
DMA = pltpu.SemaphoreType.DMA
small = pltpu.CompilerParams(vmem_limit_bytes=24 * MIB)
large = pltpu.CompilerParams(vmem_limit_bytes=60 * MIB + MIB // 2)


def whole(array):
    return pl.BlockSpec(array.shape, lambda i: (0,) * len(array.shape))


def in_hbm(*arrays):
    return [pltpu.with_memory_space_constraint(a, pltpu.HBM) for a in arrays]


def hbm(*dims, dtype=f32):
    return pltpu.HBM(dims, dtype)


def vmem(*dims, dtype=f32):
    return pltpu.VMEM(dims, dtype)


def run_plan(traces, rcv_term, cmp_term, rcv_home, cmp_home, counts):
    args = in_hbm(rcv_term.reshape(1, ROWS), cmp_term.reshape(1, ROWS),
                  rcv_home.reshape(-1, 128), cmp_home.reshape(-1, 128), traces)
    return pl.pallas_call(
        plan_kernel,
        out_shape=(vmem(DEVS, 3 * PAIR), vmem(8, ROWS)),
        in_specs=[pl.BlockSpec(memory_space=pltpu.SMEM)] + [HB] * 5,
        out_specs=(VM, VM),
        scratch_shapes=[vmem(1, ROWS, dtype=i32), vmem(1, ROWS, dtype=i32),
                        vmem(128, 128, dtype=i32), vmem(256, 128, dtype=i32),
                        vmem(ROWS, NS, dtype=bf16), DMA((8,))],
        compiler_params=small,
        name="plan",
    )(counts, *args)


def run_pick(got, rcv_filters, cmp_filters):
    return pl.pallas_call(
        pick_kernel,
        out_shape=hbm(SLOTS, TAPS),
        in_specs=[VM] * 3, out_specs=HB,
        scratch_shapes=[vmem(SLOTS, TAPS), DMA((4,))],
        compiler_params=small,
        name="pick",
    )(got, rcv_filters, cmp_filters)


def run_lags(got, traces, targets, tables):
    def blk(width):
        return pl.BlockSpec((ROWBLK, width), lambda i: (i, 0))

    return pl.pallas_call(
        lags_kernel,
        grid=(ROWS // ROWBLK,),
        out_shape=(hbm(ROWS, TAPS), hbm(ROWS, TAPS), hbm(ROWS, WIN)),
        in_specs=[pl.BlockSpec((8, 3 * PAIR), lambda i: (0, 0)), blk(NS), blk(NS)]
        + [whole(tables[n]) for n in "eic"],
        out_specs=(blk(TAPS), blk(TAPS), blk(WIN)),
        compiler_params=large,
        cost_estimate=pl.CostEstimate(flops=5 * 10 ** 9, bytes_accessed=5 * 10 ** 6,
                                      transcendentals=0),
        name="lags",
    )(*in_hbm(got, traces, targets, *[tables[n] for n in "eic"]))


def run_books(got, slot_lines, src_line, src_filters):
    int16 = jnp.int16
    out = (hbm(RCV + CMP, SLOTS, dtype=bf16), hbm(RCV + CMP, TAPS),
           hbm(ROWS, TAPS, dtype=int16), hbm(ROWS, TAPS, dtype=int16),
           hbm(48, ROWS, dtype=int16), hbm(ROWS, TAPS), hbm(16, TAPS))
    args = (got, slot_lines, src_line, src_filters)
    return pl.pallas_call(
        books_kernel,
        grid=(1,),
        out_shape=out,
        in_specs=[whole(a) for a in args], out_specs=[whole(a) for a in out],
        compiler_params=large,
        name="books",
    )(got, slot_lines, *in_hbm(*args[2:]))


def run_grad(fetched, held):
    return pl.pallas_call(
        grad_kernel,
        out_shape=(vmem(SLOTS, TAPS), vmem(SRC, TAPS)),
        in_specs=[VM] + [HB] * len(held), out_specs=(VM, VM),
        scratch_shapes=[vmem(*a.shape, dtype=a.dtype) for a in held]
        + [vmem(SLOTS, 2 * TAPS, dtype=bf16), DMA((len(held),))],
        compiler_params=small,
        name="grad",
    )(pltpu.with_memory_space_constraint(fetched, pltpu.VMEM), *in_hbm(*held))


def run_settle(back, settle_pick, energy, rcv_filters, cmp_filters, src_new):
    return pl.pallas_call(
        settle_kernel,
        out_shape=(shape(SRC, TAPS), shape(RCV, TAPS), shape(CMP, TAPS)),
        in_specs=[VM] * 6, out_specs=(VM, VM, VM),
        compiler_params=small,
        name="settle",
    )(back, settle_pick, energy, rcv_filters, cmp_filters, src_new)


def swap(rows):
    return lax.all_to_all(rows.reshape(DEVS, PAIR, TAPS), AXES, split_axis=0, concat_axis=0,
                          tiled=True).reshape(SLOTS, TAPS)


def body(traces, targets, src_local, rcv_term, cmp_term, rcv_home, cmp_home, counts,
         src_filters, rcv_filters, cmp_filters):
    tables = {name: jnp.asarray(value) for name, value in make_tables().items()}
    src_line = src_local.reshape(1, ROWS)
    pay, slot_lines = run_plan(traces, rcv_term, cmp_term, rcv_home, cmp_home, counts)
    got = lax.all_to_all(pay, AXES, split_axis=0, concat_axis=0, tiled=True)
    fetched = swap(run_pick(got, rcv_filters, cmp_filters))
    even, base, last = run_lags(got, traces, targets, tables)
    settle_pick, energy, rcol, ccol, lines, shots, scale = run_books(
        got, slot_lines, src_line, src_filters)
    send, src_new = run_grad(fetched, (rcol, ccol, shots, tables["d"], even, last, tables["tail"],
                                       tables["i"], base, lines, scale))
    return run_settle(swap(send), settle_pick, energy, rcv_filters, cmp_filters, src_new)


def solution(mesh):
    rows = P(AXES, None)
    flat = P(AXES)
    return jax.shard_map(
        body,
        mesh=mesh,
        in_specs=(rows, rows, flat, flat, flat, P(), P(), flat, rows, rows, rows),
        out_specs=(rows, rows, rows),
        check_vma=False,
    )
```

```python
import jax
import jax.numpy as jnp
import numpy as np
import ml_dtypes
from jax import lax
from jax.experimental import pallas as pl
from jax.experimental.pallas import tpu as pltpu
from jax.sharding import PartitionSpec as P

AXES = ("shot", "line")
DEVS = 128
ROWS = 512
NS = 2048
TAPS = 128
CAP = 8
PAIR = 2 * CAP
SLOTS = DEVS * PAIR
RCV = 128
CMP = 256
SRC = 4
WIN = 256
BLOCKS = NS // TAPS
ROWBLK = 256
step_size = 0.5
f32, bf16, i32 = jnp.float32, jnp.bfloat16, jnp.int32
NT = (((1,), (1,)), ((), ()))
MIB = 1024 * 1024


def split_pair(matrix):
    high = matrix.astype(ml_dtypes.bfloat16)
    low = (matrix - high.astype(np.float64)).astype(ml_dtypes.bfloat16)
    return high, low


def make_tables():
    angle = 2.0 * np.pi * (np.arange(TAPS) + 0.5) / WIN
    place = np.arange(WIN)
    phase = place[:, None] * angle[None, :]
    forward = np.concatenate([np.cos(phase), -np.sin(phase)], axis=1)
    inverse = forward.T / TAPS
    lag_phase = np.arange(TAPS)[:, None] * angle[None, :]
    even = 2.0 * np.cos(lag_phase)
    even[0] = 1.0
    d_pair = np.concatenate(split_pair(forward[:TAPS]), axis=0)
    e_pair = np.concatenate(split_pair(forward[TAPS:]), axis=0)
    i_pair = np.concatenate(split_pair(inverse[:, :TAPS]), axis=1)
    c_pair = np.concatenate(split_pair(even), axis=1)
    tail = split_pair(inverse[:, TAPS:] @ forward[TAPS:])[0]
    return dict(d=d_pair, e=e_pair, i=i_pair, c=c_pair, tail=tail)


def two(values):
    high = values.astype(bf16)
    low = (values - high.astype(f32)).astype(bf16)
    return high, low


def mm(a, b):
    return jnp.dot(a, b, preferred_element_type=f32)


def iota(shape, dim):
    return lax.broadcasted_iota(i32, shape, dim)


def as_bf16(mask):
    return mask.astype(f32).astype(bf16)


def fine_mm(values, pair):
    width = pair.shape[1] // 2
    high, low = two(values)
    both = mm(high, pair)
    return both[:, :width] + (both[:, width:] + mm(low, pair[:, :width]))


def fetch(hbm_refs, vmem_refs, sems):
    copies = [pltpu.make_async_copy(src, dst, sems.at[j])
              for j, (src, dst) in enumerate(zip(hbm_refs, vmem_refs))]
    for copy in copies:
        copy.start()
    return copies


def flag16(mask):
    return jnp.where(mask, jnp.ones(mask.shape, bf16), jnp.zeros(mask.shape, bf16))


def iota16(shape, dim):
    return lax.broadcasted_iota(jnp.int16, shape, dim)


def row16(row, count):
    tile = jnp.broadcast_to(row.astype(i32), (16, row.shape[1])).astype(jnp.int16)
    return jnp.concatenate([tile] * (count // 16), axis=0)


def plan_kernel(count_ref, rterm_hbm, cterm_hbm, rhome_hbm, chome_hbm, traces_hbm, pay_ref, slot_ref,
                rterm_ref, cterm_ref, rhome_ref, chome_ref, tbuf, sems):
    parts = [pl.ds(j * 128, 128) for j in range(4)]
    copies = fetch(
        [rterm_hbm, cterm_hbm, rhome_hbm, chome_hbm] + [traces_hbm.at[p] for p in parts],
        [rterm_ref, cterm_ref, rhome_ref, chome_ref] + [tbuf.at[p] for p in parts], sems)
    earlier = flag16(iota16((128, 128), 0) < iota16((128, 128), 1))
    count_up = jnp.concatenate([earlier, jnp.ones((128, 128), bf16)], axis=1)

    def look_up(term, home, bits):
        high, low = term >> 7, term & 127
        halves = jnp.concatenate([home >> bits, home & (2 ** bits - 1)], axis=0)
        rows = home.shape[0]
        both = mm(halves.astype(f32).astype(bf16), flag16(iota16((128, ROWS), 0) == row16(low, 128)))
        pick_high = iota((rows, ROWS), 0) == high
        return (jnp.sum(jnp.where(pick_high, both[:rows], 0.0), axis=0, keepdims=True),
                jnp.sum(jnp.where(pick_high, both[rows:], 0.0), axis=0, keepdims=True))

    for copy in copies[:4]:
        copy.wait()
    r_owner, r_place = look_up(rterm_ref[...], rhome_ref[...], 7)
    c_owner, c_place = look_up(cterm_ref[...], chome_ref[...], 8)
    for copy in copies[4:]:
        copy.wait()
    line128 = iota16((DEVS, ROWS), 0)
    mine16 = [flag16(line128 == row16(owner, DEVS)) for owner in (r_owner, c_owner)]
    mine = jnp.concatenate(mine16, axis=0)
    owners = jnp.concatenate(
        [jnp.broadcast_to(r_owner, (DEVS, ROWS)), jnp.broadcast_to(c_owner, (DEVS, ROWS))], axis=0)
    here = owners == (iota((2 * DEVS, ROWS), 0) & (DEVS - 1)).astype(f32)
    past = jnp.zeros((2 * DEVS, 128), f32)
    ranks, powers = [], []
    for j in range(4):
        part = slice(j * 128, (j + 1) * 128)
        seen = mm(mine[:, part], count_up)
        before = jnp.where(here[:, part], seen[:, :128] + past, 0.0)
        past = past + seen[:, 128:]
        ranks.append(jnp.concatenate([jnp.sum(before[:DEVS], axis=0, keepdims=True),
                                      jnp.sum(before[DEVS:], axis=0, keepdims=True)], axis=0))
        total = jnp.zeros((128, 128), f32)
        for b in range(BLOCKS):
            x = tbuf[part, b * 128:(b + 1) * 128].astype(f32)
            total = total + x * x
        powers.append(jnp.sum(jnp.transpose(total), axis=0, keepdims=True))
    rank = jnp.concatenate(ranks, axis=1)
    r_rank, c_rank = rank[0:1], rank[1:2] + CAP
    live = (iota((1, ROWS), 1) < count_ref[0]).astype(f32)
    power = jnp.concatenate(powers, axis=1) * live
    slot_ref[...] = jnp.concatenate(
        [r_owner * PAIR + r_rank, c_owner * PAIR + c_rank, live, power, jnp.zeros((4, ROWS), f32)],
        axis=0)
    p_high = power.astype(bf16).astype(f32)
    p_low = power - p_high
    line = iota((PAIR, ROWS), 0).astype(f32)

    def weights(rank, place):
        at = line == rank
        return jnp.concatenate(
            [jnp.where(at, row, 0.0) for row in (place, p_high, p_low)], axis=0).astype(bf16)

    pay_ref[...] = lax.dot_general(
        jnp.concatenate(mine16, axis=1),
        jnp.concatenate([weights(r_rank, r_place), weights(c_rank, c_place)], axis=1),
        NT, preferred_element_type=f32)


def pick_kernel(got_ref, rcv_ref, cmp_ref, out_hbm, out_ref, sems):
    pairs = [jnp.concatenate(two(t[...]), axis=1) for t in (rcv_ref, cmp_ref)]
    half = DEVS // 4
    saves = []
    for h in range(4):
        got = got_ref[h * half:(h + 1) * half, :PAIR].astype(i32)
        for side, pair in enumerate(pairs):
            lane = iota((half, pair.shape[0]), 1)
            pick = jnp.concatenate(
                [as_bf16(lane == got[:, s:s + 1]) for s in range(side * CAP, (side + 1) * CAP)], axis=0)
            both = mm(pick, pair)
            values = both[:, :TAPS] + both[:, TAPS:]
            for s in range(CAP):
                out_ref[pl.ds(h * half * PAIR + side * CAP + s, half, stride=PAIR), :] = (
                    values[s * half:(s + 1) * half])
        part = pl.ds(h * half * PAIR, half * PAIR)
        saves.append(pltpu.make_async_copy(out_ref.at[part], out_hbm.at[part], sems.at[h]))
        saves[-1].start()
    for save in saves:
        save.wait()


def lags_kernel(after_ref, traces_ref, targets_ref, e_ref, i_ref, c_ref,
                even_ref, base_ref, last_ref):
    e_pair = e_ref[...]
    sign = 1.0 - 2.0 * (iota((1, TAPS), 1) & 1).astype(f32)
    own = [jnp.zeros((ROWBLK, TAPS), f32)] * 2
    cross = [jnp.zeros((ROWBLK, TAPS), f32)] * 2
    back = None
    for b in range(BLOCKS):
        now = traces_ref[:, b * 128:(b + 1) * 128]
        goal = targets_ref[:, b * 128:(b + 1) * 128]
        u = mm(jnp.concatenate([now, now], axis=1), e_pair)
        v = mm(jnp.concatenate([goal, goal], axis=1), e_pair)
        ur, ui = u[:, :TAPS], u[:, TAPS:]
        vr, vi = v[:, :TAPS], v[:, TAPS:]
        xr, xi = (ur, ui) if b == 0 else (ur + back[0], ui + back[1])
        own = [own[0] + (xr * ur + xi * ui), own[1] + (xr * ui - xi * ur)]
        cross = [cross[0] + (xr * vr + xi * vi), cross[1] + (xr * vi - xi * vr)]
        back = -sign * ui, sign * ur
    i_pair = i_ref[...]
    even_ref[...] = fine_mm(fine_mm(jnp.concatenate(own, axis=1), i_pair), c_ref[...])
    base_ref[...] = fine_mm(jnp.concatenate(cross, axis=1), i_pair)
    last_ref[...] = jnp.concatenate(back, axis=1)


def books_kernel(got_ref, slot_ref, srcloc_ref, src_ref,
                 settle_ref, energy_ref, rcol_ref, ccol_ref, line_ref, shot_ref, scale_ref):
    got = jnp.concatenate([got_ref[...], jnp.zeros((DEVS, 128 - 3 * PAIR), f32)], axis=1)
    turned = jnp.transpose(got)[:3 * PAIR].astype(bf16)
    half = DEVS * CAP
    spread = as_bf16((iota((DEVS, half), 1) >> 3) == iota((DEVS, half), 0))
    wide = mm(turned, spread)
    here = iota((CAP, half), 0) == (iota((CAP, half), 1) & (CAP - 1))

    def line_of(values):
        return jnp.sum(jnp.where(here, values, 0.0), axis=0, keepdims=True)

    for side, (start, count) in enumerate(((0, RCV), (RCV, CMP))):
        row = side * CAP
        place = line_of(wide[row:row + CAP]).astype(i32)
        power = line_of(wide[PAIR + row:PAIR + row + CAP] + wide[2 * PAIR + row:2 * PAIR + row + CAP])
        for c in range(count // 128):
            part = slice(start + c * 128, start + (c + 1) * 128)
            hit = iota((128, half), 0) + c * 128 == place
            settle_ref[part, :] = as_bf16(hit)
            energy = jnp.sum(jnp.where(hit, power, 0.0), axis=1, keepdims=True)
            energy_ref[part, :] = jnp.broadcast_to(step_size / jnp.maximum(energy, 1.0), (128, 128))
    lines = jnp.concatenate(
        [slot_ref[...], srcloc_ref[...].astype(f32), jnp.zeros((128 - 9, ROWS), f32)], axis=0)
    src = src_ref[...]
    for j in range(4):
        part = slice(j * 128, (j + 1) * 128)
        col = jnp.transpose(lines[:, part])
        rcol_ref[part, :] = jnp.broadcast_to(col[:, 0:1].astype(i32), (128, 128)).astype(jnp.int16)
        ccol_ref[part, :] = jnp.broadcast_to(col[:, 1:2].astype(i32), (128, 128)).astype(jnp.int16)
        src_rows = jnp.zeros((128, TAPS), f32)
        for s in range(SRC):
            src_rows = jnp.where(col[:, 8:9] == float(s), src[s:s + 1, :], src_rows)
        shot_ref[part, :] = src_rows
    live = slot_ref[2:3, :] > 0.0
    for j, row in enumerate((slot_ref[0:1, :], slot_ref[1:2, :], srcloc_ref[...].astype(f32))):
        line_ref[16 * j:16 * (j + 1), :] = jnp.broadcast_to(
            jnp.where(live, row, -1.0).astype(i32), (16, ROWS)).astype(jnp.int16)
    mine = iota((8, ROWS), 0) == srcloc_ref[...]
    energy = jnp.sum(jnp.where(mine, slot_ref[3:4, :], 0.0), axis=1, keepdims=True)
    scale_ref[:8, :] = jnp.broadcast_to(step_size / jnp.maximum(energy, 1.0), (8, TAPS))
    scale_ref[8:, :] = jnp.concatenate([src, jnp.zeros((8 - SRC, TAPS), f32)], axis=0)


def one_hot16(at, first, second):
    ones = jnp.ones(at.shape, bf16)
    return jnp.where((at == first) | (at == second), ones, jnp.zeros(at.shape, bf16))


def grad_kernel(fetched_ref, *refs):
    hbm_refs, (out_ref, src_out_ref) = refs[:11], refs[11:13]
    vmem_refs, rows_ref, sems = refs[13:24], refs[24], refs[25]
    copies = fetch(hbm_refs, vmem_refs, sems)
    (rcol_ref, ccol_ref, shot_ref, d_ref, even_ref, last_ref, tail_ref, i_ref, base_ref,
     line_ref, scale_ref) = vmem_refs
    chunk = 512
    chunks = SLOTS // chunk
    lane = iota16((ROWS, 128), 1)
    for k in range(chunks):
        part = slice(k * chunk, (k + 1) * chunk)
        rows_ref[part, :] = jnp.concatenate(two(fetched_ref[part, :]), axis=1)
    for copy in copies[:2]:
        copy.wait()
    rcol, ccol = rcol_ref[...], ccol_ref[...]
    both = None
    for k in range(chunks):
        pick = jnp.concatenate(
            [one_hot16(lane + jnp.int16(k * chunk + j * 128), rcol, ccol) for j in range(chunk // 128)],
            axis=1)
        part = mm(pick, rows_ref[k * chunk:(k + 1) * chunk, :])
        both = part if k == 0 else both + part
    for copy in copies[2:]:
        copy.wait()
    mixed = (shot_ref[...] + (both[:, :TAPS] + both[:, TAPS:])).astype(bf16)
    h = mm(jnp.concatenate([mixed, mixed], axis=1), d_ref[...])
    hr, hi = h[:, :TAPS], h[:, TAPS:]
    xr, xi = last_ref[:, :TAPS], last_ref[:, TAPS:]
    past = jnp.concatenate([xr * hr - xi * hi, xr * hi + xi * hr], axis=1)
    m = mm(past.astype(bf16), tail_ref[...])
    mr, mi = m[:, :TAPS], m[:, TAPS:]
    even = even_ref[...]
    spectrum = jnp.concatenate(
        [even * hr - (xr * mr + xi * mi), even * hi - (xr * mi - xi * mr)], axis=1)
    grad = fine_mm(spectrum, i_ref[...]) - base_ref[...]
    rows = jnp.concatenate(two(grad), axis=1)
    first = jnp.concatenate([line_ref[:16, :]] * (chunk // 16), axis=0)
    second = jnp.concatenate([line_ref[16:32, :]] * (chunk // 16), axis=0)
    for k in range(chunks):
        at = iota16((chunk, ROWS), 0) + jnp.int16(k * chunk)
        both = mm(one_hot16(at, first, second), rows)
        out_ref[k * chunk:(k + 1) * chunk, :] = both[:, :TAPS] + both[:, TAPS:]
    both = mm(flag16(iota16((16, ROWS), 0) == line_ref[32:, :]), rows)
    src_out_ref[...] = scale_ref[8:8 + SRC, :] - ((both[:8, :TAPS] + both[:8, TAPS:])
                                                  * scale_ref[:8, :])[:SRC]


def settle_kernel(grads_ref, pick_ref, energy_ref, rcv_ref, cmp_ref, src_ref,
                  src_out_ref, rcv_out_ref, cmp_out_ref):
    src_out_ref[...] = src_ref[...]
    sides = grads_ref[...].reshape(DEVS, 2, CAP, TAPS)
    for side, part, table_ref, out_ref in ((0, slice(0, RCV), rcv_ref, rcv_out_ref),
                                           (1, slice(RCV, RCV + CMP), cmp_ref, cmp_out_ref)):
        rows = jnp.concatenate(two(sides[:, side].reshape(DEVS * CAP, TAPS)), axis=1)
        total = mm(pick_ref[part, :], rows)
        out_ref[...] = table_ref[...] - (total[:, :TAPS] + total[:, TAPS:]) * energy_ref[part, :]


def shape(*dims, dtype=f32):
    return jax.ShapeDtypeStruct(dims, dtype)


VM = pl.BlockSpec(memory_space=pltpu.VMEM)
HB = pl.BlockSpec(memory_space=pltpu.HBM)
DMA = pltpu.SemaphoreType.DMA
small = pltpu.CompilerParams(vmem_limit_bytes=24 * MIB)
large = pltpu.CompilerParams(vmem_limit_bytes=60 * MIB + MIB // 2)


def whole(array):
    return pl.BlockSpec(array.shape, lambda i: (0,) * len(array.shape))


def in_hbm(*arrays):
    return [pltpu.with_memory_space_constraint(a, pltpu.HBM) for a in arrays]


def hbm(*dims, dtype=f32):
    return pltpu.HBM(dims, dtype)


def vmem(*dims, dtype=f32):
    return pltpu.VMEM(dims, dtype)


def run_plan(traces, rcv_term, cmp_term, rcv_home, cmp_home, counts):
    args = in_hbm(rcv_term.reshape(1, ROWS), cmp_term.reshape(1, ROWS),
                  rcv_home.reshape(-1, 128), cmp_home.reshape(-1, 128), traces)
    return pl.pallas_call(
        plan_kernel,
        out_shape=(vmem(DEVS, 3 * PAIR), vmem(8, ROWS)),
        in_specs=[pl.BlockSpec(memory_space=pltpu.SMEM)] + [HB] * 5,
        out_specs=(VM, VM),
        scratch_shapes=[vmem(1, ROWS, dtype=i32), vmem(1, ROWS, dtype=i32),
                        vmem(128, 128, dtype=i32), vmem(256, 128, dtype=i32),
                        vmem(ROWS, NS, dtype=bf16), DMA((8,))],
        compiler_params=small,
        name="plan",
    )(counts, *args)


def run_pick(got, rcv_filters, cmp_filters):
    return pl.pallas_call(
        pick_kernel,
        out_shape=hbm(SLOTS, TAPS),
        in_specs=[VM] * 3, out_specs=HB,
        scratch_shapes=[vmem(SLOTS, TAPS), DMA((4,))],
        compiler_params=small,
        name="pick",
    )(got, rcv_filters, cmp_filters)


def run_lags(got, traces, targets, tables):
    def blk(width):
        return pl.BlockSpec((ROWBLK, width), lambda i: (i, 0))

    return pl.pallas_call(
        lags_kernel,
        grid=(ROWS // ROWBLK,),
        out_shape=(hbm(ROWS, TAPS), hbm(ROWS, TAPS), hbm(ROWS, WIN)),
        in_specs=[pl.BlockSpec((8, 3 * PAIR), lambda i: (0, 0)), blk(NS), blk(NS)]
        + [whole(tables[n]) for n in "eic"],
        out_specs=(blk(TAPS), blk(TAPS), blk(WIN)),
        compiler_params=large,
        cost_estimate=pl.CostEstimate(flops=5 * 10 ** 9, bytes_accessed=5 * 10 ** 6,
                                      transcendentals=0),
        name="lags",
    )(*in_hbm(got, traces, targets, *[tables[n] for n in "eic"]))


def run_books(got, slot_lines, src_line, src_filters):
    int16 = jnp.int16
    out = (hbm(RCV + CMP, DEVS * CAP, dtype=bf16), hbm(RCV + CMP, TAPS),
           hbm(ROWS, TAPS, dtype=int16), hbm(ROWS, TAPS, dtype=int16),
           hbm(48, ROWS, dtype=int16), hbm(ROWS, TAPS), hbm(16, TAPS))
    args = (got, slot_lines, src_line, src_filters)
    return pl.pallas_call(
        books_kernel,
        grid=(1,),
        out_shape=out,
        in_specs=[whole(a) for a in args], out_specs=[whole(a) for a in out],
        compiler_params=large,
        name="books",
    )(got, slot_lines, *in_hbm(*args[2:]))


def run_grad(fetched, held):
    return pl.pallas_call(
        grad_kernel,
        out_shape=(vmem(SLOTS, TAPS), vmem(SRC, TAPS)),
        in_specs=[VM] + [HB] * len(held), out_specs=(VM, VM),
        scratch_shapes=[vmem(*a.shape, dtype=a.dtype) for a in held]
        + [vmem(SLOTS, 2 * TAPS, dtype=bf16), DMA((len(held),))],
        compiler_params=small,
        name="grad",
    )(pltpu.with_memory_space_constraint(fetched, pltpu.VMEM), *in_hbm(*held))


def run_settle(back, settle_pick, energy, rcv_filters, cmp_filters, src_new):
    return pl.pallas_call(
        settle_kernel,
        out_shape=(shape(SRC, TAPS), shape(RCV, TAPS), shape(CMP, TAPS)),
        in_specs=[VM] * 6, out_specs=(VM, VM, VM),
        compiler_params=small,
        name="settle",
    )(back, settle_pick, energy, rcv_filters, cmp_filters, src_new)


def swap(rows):
    return lax.all_to_all(rows.reshape(DEVS, PAIR, TAPS), AXES, split_axis=0, concat_axis=0,
                          tiled=True).reshape(SLOTS, TAPS)


def body(traces, targets, src_local, rcv_term, cmp_term, rcv_home, cmp_home, counts,
         src_filters, rcv_filters, cmp_filters):
    tables = {name: jnp.asarray(value) for name, value in make_tables().items()}
    src_line = src_local.reshape(1, ROWS)
    pay, slot_lines = run_plan(traces, rcv_term, cmp_term, rcv_home, cmp_home, counts)
    got = lax.all_to_all(pay, AXES, split_axis=0, concat_axis=0, tiled=True)
    fetched = swap(run_pick(got, rcv_filters, cmp_filters))
    even, base, last = run_lags(got, traces, targets, tables)
    settle_pick, energy, rcol, ccol, lines, shots, scale = run_books(
        got, slot_lines, src_line, src_filters)
    send, src_new = run_grad(fetched, (rcol, ccol, shots, tables["d"], even, last, tables["tail"],
                                       tables["i"], base, lines, scale))
    return run_settle(swap(send), settle_pick, energy, rcv_filters, cmp_filters, src_new)


def solution(mesh):
    rows = P(AXES, None)
    flat = P(AXES)
    return jax.shard_map(
        body,
        mesh=mesh,
        in_specs=(rows, rows, flat, flat, flat, P(), P(), flat, rows, rows, rows),
        out_specs=(rows, rows, rows),
        check_vma=False,
    )
```

```python
import jax
import jax.numpy as jnp
import numpy as np
import ml_dtypes
from jax import lax
from jax.experimental import pallas as pl
from jax.experimental.pallas import tpu as pltpu
from jax.sharding import PartitionSpec as P

AXES = ("shot", "line")
DEVS = 128
ROWS = 512
NS = 2048
TAPS = 128
CAP = 8
PAIR = 2 * CAP
SLOTS = DEVS * PAIR
RCV = 128
CMP = 256
SRC = 4
WIN = 256
BLOCKS = NS // TAPS
ROWBLK = 256
step_size = 0.5
f32, bf16, i32 = jnp.float32, jnp.bfloat16, jnp.int32
NT = (((1,), (1,)), ((), ()))
MIB = 1024 * 1024


def split_pair(matrix):
    high = matrix.astype(ml_dtypes.bfloat16)
    low = (matrix - high.astype(np.float64)).astype(ml_dtypes.bfloat16)
    return high, low


def make_tables():
    angle = 2.0 * np.pi * (np.arange(TAPS) + 0.5) / WIN
    place = np.arange(WIN)
    phase = place[:, None] * angle[None, :]
    forward = np.concatenate([np.cos(phase), -np.sin(phase)], axis=1)
    inverse = forward.T / TAPS
    lag_phase = np.arange(TAPS)[:, None] * angle[None, :]
    even = 2.0 * np.cos(lag_phase)
    even[0] = 1.0
    d_pair = np.concatenate(split_pair(forward[:TAPS]), axis=0)
    e_pair = np.concatenate(split_pair(forward[TAPS:]), axis=0)
    i_pair = np.concatenate(split_pair(inverse[:, :TAPS]), axis=1)
    c_pair = np.concatenate(split_pair(even), axis=1)
    tail = np.concatenate(split_pair(inverse[:, TAPS:] @ forward[TAPS:]), axis=1)
    return dict(d=d_pair, e=e_pair, i=i_pair, c=c_pair, tail=tail)


def two(values):
    high = values.astype(bf16)
    low = (values - high.astype(f32)).astype(bf16)
    return high, low


def mm(a, b):
    return jnp.dot(a, b, preferred_element_type=f32)


def iota(shape, dim):
    return lax.broadcasted_iota(i32, shape, dim)


def as_bf16(mask):
    return mask.astype(f32).astype(bf16)


def fine_mm(values, pair):
    width = pair.shape[1] // 2
    high, low = two(values)
    both = mm(high, pair)
    return both[:, :width] + (both[:, width:] + mm(low, pair[:, :width]))


def fetch(hbm_refs, vmem_refs, sems):
    copies = [pltpu.make_async_copy(src, dst, sems.at[j])
              for j, (src, dst) in enumerate(zip(hbm_refs, vmem_refs))]
    for copy in copies:
        copy.start()
    return copies


def flag16(mask):
    return jnp.where(mask, jnp.ones(mask.shape, bf16), jnp.zeros(mask.shape, bf16))


def iota16(shape, dim):
    return lax.broadcasted_iota(jnp.int16, shape, dim)


def row16(row, count):
    tile = jnp.broadcast_to(row.astype(i32), (16, row.shape[1])).astype(jnp.int16)
    return jnp.concatenate([tile] * (count // 16), axis=0)


def plan_kernel(count_ref, rterm_hbm, cterm_hbm, rhome_hbm, chome_hbm, traces_hbm, pay_ref, slot_ref,
                rterm_ref, cterm_ref, rhome_ref, chome_ref, tbuf, sems):
    parts = [pl.ds(j * 128, 128) for j in range(4)]
    copies = fetch(
        [rterm_hbm, cterm_hbm, rhome_hbm, chome_hbm] + [traces_hbm.at[p] for p in parts],
        [rterm_ref, cterm_ref, rhome_ref, chome_ref] + [tbuf.at[p] for p in parts], sems)
    earlier = flag16(iota16((128, 128), 0) < iota16((128, 128), 1))
    count_up = jnp.concatenate([earlier, jnp.ones((128, 128), bf16)], axis=1)

    def look_up(term, home, bits):
        high, low = term >> 7, term & 127
        halves = jnp.concatenate([home >> bits, home & (2 ** bits - 1)], axis=0)
        rows = home.shape[0]
        both = mm(halves.astype(f32).astype(bf16), flag16(iota16((128, ROWS), 0) == row16(low, 128)))
        pick_high = iota((rows, ROWS), 0) == high
        return (jnp.sum(jnp.where(pick_high, both[:rows], 0.0), axis=0, keepdims=True),
                jnp.sum(jnp.where(pick_high, both[rows:], 0.0), axis=0, keepdims=True))

    for copy in copies[:4]:
        copy.wait()
    r_owner, r_place = look_up(rterm_ref[...], rhome_ref[...], 7)
    c_owner, c_place = look_up(cterm_ref[...], chome_ref[...], 8)
    for copy in copies[4:]:
        copy.wait()
    line128 = iota16((DEVS, ROWS), 0)
    mine16 = [flag16(line128 == row16(owner, DEVS)) for owner in (r_owner, c_owner)]
    mine = jnp.concatenate(mine16, axis=0)
    owners = jnp.concatenate(
        [jnp.broadcast_to(r_owner, (DEVS, ROWS)), jnp.broadcast_to(c_owner, (DEVS, ROWS))], axis=0)
    here = owners == (iota((2 * DEVS, ROWS), 0) & (DEVS - 1)).astype(f32)
    past = jnp.zeros((2 * DEVS, 128), f32)
    ranks, powers = [], []
    for j in range(4):
        part = slice(j * 128, (j + 1) * 128)
        seen = mm(mine[:, part], count_up)
        before = jnp.where(here[:, part], seen[:, :128] + past, 0.0)
        past = past + seen[:, 128:]
        ranks.append(jnp.concatenate([jnp.sum(before[:DEVS], axis=0, keepdims=True),
                                      jnp.sum(before[DEVS:], axis=0, keepdims=True)], axis=0))
        total = jnp.zeros((128, 128), f32)
        for b in range(BLOCKS):
            x = tbuf[part, b * 128:(b + 1) * 128].astype(f32)
            total = total + x * x
        powers.append(jnp.sum(jnp.transpose(total), axis=0, keepdims=True))
    rank = jnp.concatenate(ranks, axis=1)
    r_rank, c_rank = rank[0:1], rank[1:2] + CAP
    live = (iota((1, ROWS), 1) < count_ref[0]).astype(f32)
    power = jnp.concatenate(powers, axis=1) * live
    slot_ref[...] = jnp.concatenate(
        [r_owner * PAIR + r_rank, c_owner * PAIR + c_rank, live, power, jnp.zeros((4, ROWS), f32)],
        axis=0)
    p_high = power.astype(bf16).astype(f32)
    p_low = power - p_high
    line = iota((PAIR, ROWS), 0).astype(f32)

    def weights(rank, place):
        at = line == rank
        return jnp.concatenate(
            [jnp.where(at, row, 0.0) for row in (place, p_high, p_low)], axis=0).astype(bf16)

    pay_ref[...] = lax.dot_general(
        jnp.concatenate(mine16, axis=1),
        jnp.concatenate([weights(r_rank, r_place), weights(c_rank, c_place)], axis=1),
        NT, preferred_element_type=f32)


def pick_kernel(got_ref, rcv_ref, cmp_ref, out_hbm, out_ref, sems):
    pairs = [jnp.concatenate(two(t[...]), axis=1) for t in (rcv_ref, cmp_ref)]
    half = DEVS // 4
    saves = []
    for h in range(4):
        got = got_ref[h * half:(h + 1) * half, :PAIR].astype(i32)
        for side, pair in enumerate(pairs):
            lane = iota((half, pair.shape[0]), 1)
            pick = jnp.concatenate(
                [as_bf16(lane == got[:, s:s + 1]) for s in range(side * CAP, (side + 1) * CAP)], axis=0)
            both = mm(pick, pair)
            values = both[:, :TAPS] + both[:, TAPS:]
            for s in range(CAP):
                out_ref[pl.ds(h * half * PAIR + side * CAP + s, half, stride=PAIR), :] = (
                    values[s * half:(s + 1) * half])
        part = pl.ds(h * half * PAIR, half * PAIR)
        saves.append(pltpu.make_async_copy(out_ref.at[part], out_hbm.at[part], sems.at[h]))
        saves[-1].start()
    for save in saves:
        save.wait()


def lags_kernel(after_ref, traces_ref, targets_ref, e_ref, i_ref, c_ref,
                even_ref, base_ref, last_ref):
    e_pair = e_ref[...]
    sign = 1.0 - 2.0 * (iota((1, TAPS), 1) & 1).astype(f32)
    own = [jnp.zeros((ROWBLK, TAPS), f32)] * 2
    cross = [jnp.zeros((ROWBLK, TAPS), f32)] * 2
    back = None
    for b in range(BLOCKS):
        now = traces_ref[:, b * 128:(b + 1) * 128]
        goal = targets_ref[:, b * 128:(b + 1) * 128]
        u = mm(jnp.concatenate([now, now], axis=1), e_pair)
        v = mm(jnp.concatenate([goal, goal], axis=1), e_pair)
        ur, ui = u[:, :TAPS], u[:, TAPS:]
        vr, vi = v[:, :TAPS], v[:, TAPS:]
        xr, xi = (ur, ui) if b == 0 else (ur + back[0], ui + back[1])
        own = [own[0] + (xr * ur + xi * ui), own[1] + (xr * ui - xi * ur)]
        cross = [cross[0] + (xr * vr + xi * vi), cross[1] + (xr * vi - xi * vr)]
        back = -sign * ui, sign * ur
    i_pair = i_ref[...]
    even_ref[...] = fine_mm(fine_mm(jnp.concatenate(own, axis=1), i_pair), c_ref[...])
    base_ref[...] = fine_mm(jnp.concatenate(cross, axis=1), i_pair)
    last_ref[...] = jnp.concatenate(back, axis=1)


def books_kernel(got_ref, slot_ref, srcloc_ref, src_ref,
                 settle_ref, energy_ref, rcol_ref, ccol_ref, line_ref, shot_ref, scale_ref):
    got = jnp.concatenate([got_ref[...], jnp.zeros((DEVS, 128 - 3 * PAIR), f32)], axis=1)
    turned = jnp.transpose(got)[:3 * PAIR].astype(bf16)
    half = DEVS * CAP
    spread = as_bf16((iota((DEVS, half), 1) >> 3) == iota((DEVS, half), 0))
    wide = mm(turned, spread)
    here = iota((CAP, half), 0) == (iota((CAP, half), 1) & (CAP - 1))

    def line_of(values):
        return jnp.sum(jnp.where(here, values, 0.0), axis=0, keepdims=True)

    for side, (start, count) in enumerate(((0, RCV), (RCV, CMP))):
        row = side * CAP
        place = line_of(wide[row:row + CAP]).astype(i32)
        power = line_of(wide[PAIR + row:PAIR + row + CAP] + wide[2 * PAIR + row:2 * PAIR + row + CAP])
        for c in range(count // 128):
            part = slice(start + c * 128, start + (c + 1) * 128)
            hit = iota((128, half), 0) + c * 128 == place
            settle_ref[part, :] = as_bf16(hit)
            energy = jnp.sum(jnp.where(hit, power, 0.0), axis=1, keepdims=True)
            energy_ref[part, :] = jnp.broadcast_to(step_size / jnp.maximum(energy, 1.0), (128, 128))
    lines = jnp.concatenate(
        [slot_ref[...], srcloc_ref[...].astype(f32), jnp.zeros((128 - 9, ROWS), f32)], axis=0)
    src = src_ref[...]
    for j in range(4):
        part = slice(j * 128, (j + 1) * 128)
        col = jnp.transpose(lines[:, part])
        rcol_ref[part, :] = jnp.broadcast_to(col[:, 0:1].astype(i32), (128, 128)).astype(jnp.int16)
        ccol_ref[part, :] = jnp.broadcast_to(col[:, 1:2].astype(i32), (128, 128)).astype(jnp.int16)
        src_rows = jnp.zeros((128, TAPS), f32)
        for s in range(SRC):
            src_rows = jnp.where(col[:, 8:9] == float(s), src[s:s + 1, :], src_rows)
        shot_ref[part, :] = src_rows
    live = slot_ref[2:3, :] > 0.0
    for j, row in enumerate((slot_ref[0:1, :], slot_ref[1:2, :], srcloc_ref[...].astype(f32))):
        line_ref[16 * j:16 * (j + 1), :] = jnp.broadcast_to(
            jnp.where(live, row, -1.0).astype(i32), (16, ROWS)).astype(jnp.int16)
    mine = iota((8, ROWS), 0) == srcloc_ref[...]
    energy = jnp.sum(jnp.where(mine, slot_ref[3:4, :], 0.0), axis=1, keepdims=True)
    scale_ref[:8, :] = jnp.broadcast_to(step_size / jnp.maximum(energy, 1.0), (8, TAPS))
    scale_ref[8:, :] = jnp.concatenate([src, jnp.zeros((8 - SRC, TAPS), f32)], axis=0)


def one_hot16(at, first, second):
    ones = jnp.ones(at.shape, bf16)
    return jnp.where((at == first) | (at == second), ones, jnp.zeros(at.shape, bf16))


def grad_kernel(fetched_ref, *refs):
    hbm_refs, (out_ref, src_out_ref) = refs[:11], refs[11:13]
    vmem_refs, rows_ref, sems = refs[13:24], refs[24], refs[25]
    copies = fetch(hbm_refs, vmem_refs, sems)
    (rcol_ref, ccol_ref, shot_ref, d_ref, even_ref, last_ref, tail_ref, i_ref, base_ref,
     line_ref, scale_ref) = vmem_refs
    chunk = 512
    chunks = SLOTS // chunk
    lane = iota16((ROWS, 128), 1)
    for k in range(chunks):
        part = slice(k * chunk, (k + 1) * chunk)
        rows_ref[part, :] = jnp.concatenate(two(fetched_ref[part, :]), axis=1)
    for copy in copies[:2]:
        copy.wait()
    rcol, ccol = rcol_ref[...], ccol_ref[...]
    both = None
    for k in range(chunks):
        pick = jnp.concatenate(
            [one_hot16(lane + jnp.int16(k * chunk + j * 128), rcol, ccol) for j in range(chunk // 128)],
            axis=1)
        part = mm(pick, rows_ref[k * chunk:(k + 1) * chunk, :])
        both = part if k == 0 else both + part
    for copy in copies[2:]:
        copy.wait()
    mixed = (shot_ref[...] + (both[:, :TAPS] + both[:, TAPS:])).astype(bf16)
    h = mm(jnp.concatenate([mixed, mixed], axis=1), d_ref[...])
    hr, hi = h[:, :TAPS], h[:, TAPS:]
    xr, xi = last_ref[:, :TAPS], last_ref[:, TAPS:]
    past = jnp.concatenate([xr * hr - xi * hi, xr * hi + xi * hr], axis=1)
    m = fine_mm(past, tail_ref[...])
    mr, mi = m[:, :TAPS], m[:, TAPS:]
    even = even_ref[...]
    spectrum = jnp.concatenate(
        [even * hr - (xr * mr + xi * mi), even * hi - (xr * mi - xi * mr)], axis=1)
    grad = fine_mm(spectrum, i_ref[...]) - base_ref[...]
    rows = jnp.concatenate(two(grad), axis=1)
    first = jnp.concatenate([line_ref[:16, :]] * (chunk // 16), axis=0)
    second = jnp.concatenate([line_ref[16:32, :]] * (chunk // 16), axis=0)
    for k in range(chunks):
        at = iota16((chunk, ROWS), 0) + jnp.int16(k * chunk)
        both = mm(one_hot16(at, first, second), rows)
        out_ref[k * chunk:(k + 1) * chunk, :] = both[:, :TAPS] + both[:, TAPS:]
    both = mm(flag16(iota16((16, ROWS), 0) == line_ref[32:, :]), rows)
    src_out_ref[...] = scale_ref[8:8 + SRC, :] - ((both[:8, :TAPS] + both[:8, TAPS:])
                                                  * scale_ref[:8, :])[:SRC]


def settle_kernel(grads_ref, pick_ref, energy_ref, rcv_ref, cmp_ref, src_ref,
                  src_out_ref, rcv_out_ref, cmp_out_ref):
    src_out_ref[...] = src_ref[...]
    sides = grads_ref[...].reshape(DEVS, 2, CAP, TAPS)
    for side, part, table_ref, out_ref in ((0, slice(0, RCV), rcv_ref, rcv_out_ref),
                                           (1, slice(RCV, RCV + CMP), cmp_ref, cmp_out_ref)):
        rows = jnp.concatenate(two(sides[:, side].reshape(DEVS * CAP, TAPS)), axis=1)
        total = mm(pick_ref[part, :], rows)
        out_ref[...] = table_ref[...] - (total[:, :TAPS] + total[:, TAPS:]) * energy_ref[part, :]


def shape(*dims, dtype=f32):
    return jax.ShapeDtypeStruct(dims, dtype)


VM = pl.BlockSpec(memory_space=pltpu.VMEM)
HB = pl.BlockSpec(memory_space=pltpu.HBM)
DMA = pltpu.SemaphoreType.DMA
small = pltpu.CompilerParams(vmem_limit_bytes=24 * MIB)
large = pltpu.CompilerParams(vmem_limit_bytes=60 * MIB + MIB // 2)


def whole(array):
    return pl.BlockSpec(array.shape, lambda i: (0,) * len(array.shape))


def in_hbm(*arrays):
    return [pltpu.with_memory_space_constraint(a, pltpu.HBM) for a in arrays]


def hbm(*dims, dtype=f32):
    return pltpu.HBM(dims, dtype)


def vmem(*dims, dtype=f32):
    return pltpu.VMEM(dims, dtype)


def run_plan(traces, rcv_term, cmp_term, rcv_home, cmp_home, counts):
    args = in_hbm(rcv_term.reshape(1, ROWS), cmp_term.reshape(1, ROWS),
                  rcv_home.reshape(-1, 128), cmp_home.reshape(-1, 128), traces)
    return pl.pallas_call(
        plan_kernel,
        out_shape=(vmem(DEVS, 3 * PAIR), vmem(8, ROWS)),
        in_specs=[pl.BlockSpec(memory_space=pltpu.SMEM)] + [HB] * 5,
        out_specs=(VM, VM),
        scratch_shapes=[vmem(1, ROWS, dtype=i32), vmem(1, ROWS, dtype=i32),
                        vmem(128, 128, dtype=i32), vmem(256, 128, dtype=i32),
                        vmem(ROWS, NS, dtype=bf16), DMA((8,))],
        compiler_params=small,
        name="plan",
    )(counts, *args)


def run_pick(got, rcv_filters, cmp_filters):
    return pl.pallas_call(
        pick_kernel,
        out_shape=hbm(SLOTS, TAPS),
        in_specs=[VM] * 3, out_specs=HB,
        scratch_shapes=[vmem(SLOTS + DEVS, TAPS), DMA((4,))],
        compiler_params=small,
        name="pick",
    )(got, rcv_filters, cmp_filters)


def run_lags(got, traces, targets, tables):
    def blk(width):
        return pl.BlockSpec((ROWBLK, width), lambda i: (i, 0))

    return pl.pallas_call(
        lags_kernel,
        grid=(ROWS // ROWBLK,),
        out_shape=(hbm(ROWS, TAPS), hbm(ROWS, TAPS), hbm(ROWS, WIN)),
        in_specs=[pl.BlockSpec((8, 3 * PAIR), lambda i: (0, 0)), blk(NS), blk(NS)]
        + [whole(tables[n]) for n in "eic"],
        out_specs=(blk(TAPS), blk(TAPS), blk(WIN)),
        compiler_params=large,
        cost_estimate=pl.CostEstimate(flops=5 * 10 ** 9, bytes_accessed=5 * 10 ** 6,
                                      transcendentals=0),
        name="lags",
    )(*in_hbm(got, traces, targets, *[tables[n] for n in "eic"]))


def run_books(got, slot_lines, src_line, src_filters):
    int16 = jnp.int16
    out = (hbm(RCV + CMP, DEVS * CAP, dtype=bf16), hbm(RCV + CMP, TAPS),
           hbm(ROWS, TAPS, dtype=int16), hbm(ROWS, TAPS, dtype=int16),
           hbm(48, ROWS, dtype=int16), hbm(ROWS, TAPS), hbm(16, TAPS))
    args = (got, slot_lines, src_line, src_filters)
    return pl.pallas_call(
        books_kernel,
        grid=(1,),
        out_shape=out,
        in_specs=[whole(a) for a in args], out_specs=[whole(a) for a in out],
        compiler_params=large,
        name="books",
    )(got, slot_lines, *in_hbm(*args[2:]))


def run_grad(fetched, held):
    return pl.pallas_call(
        grad_kernel,
        out_shape=(vmem(SLOTS, TAPS), vmem(SRC, TAPS)),
        in_specs=[VM] + [HB] * len(held), out_specs=(VM, VM),
        scratch_shapes=[vmem(*a.shape, dtype=a.dtype) for a in held]
        + [vmem(SLOTS, 2 * TAPS, dtype=bf16), DMA((len(held),))],
        compiler_params=small,
        name="grad",
    )(pltpu.with_memory_space_constraint(fetched, pltpu.VMEM), *in_hbm(*held))


def run_settle(back, settle_pick, energy, rcv_filters, cmp_filters, src_new):
    return pl.pallas_call(
        settle_kernel,
        out_shape=(shape(SRC, TAPS), shape(RCV, TAPS), shape(CMP, TAPS)),
        in_specs=[VM] * 6, out_specs=(VM, VM, VM),
        compiler_params=small,
        name="settle",
    )(back, settle_pick, energy, rcv_filters, cmp_filters, src_new)


def swap(rows):
    return lax.all_to_all(rows.reshape(DEVS, PAIR, TAPS), AXES, split_axis=0, concat_axis=0,
                          tiled=True).reshape(SLOTS, TAPS)


def body(traces, targets, src_local, rcv_term, cmp_term, rcv_home, cmp_home, counts,
         src_filters, rcv_filters, cmp_filters):
    tables = {name: jnp.asarray(value) for name, value in make_tables().items()}
    src_line = src_local.reshape(1, ROWS)
    pay, slot_lines = run_plan(traces, rcv_term, cmp_term, rcv_home, cmp_home, counts)
    got = lax.all_to_all(pay, AXES, split_axis=0, concat_axis=0, tiled=True)
    fetched = swap(run_pick(got, rcv_filters, cmp_filters))
    even, base, last = run_lags(got, traces, targets, tables)
    settle_pick, energy, rcol, ccol, lines, shots, scale = run_books(
        got, slot_lines, src_line, src_filters)
    send, src_new = run_grad(fetched, (rcol, ccol, shots, tables["d"], even, last, tables["tail"],
                                       tables["i"], base, lines, scale))
    return run_settle(swap(send), settle_pick, energy, rcv_filters, cmp_filters, src_new)


def solution(mesh):
    rows = P(AXES, None)
    flat = P(AXES)
    return jax.shard_map(
        body,
        mesh=mesh,
        in_specs=(rows, rows, flat, flat, flat, P(), P(), flat, rows, rows, rows),
        out_specs=(rows, rows, rows),
        check_vma=False,
    )
```

```python
import jax
import jax.numpy as jnp
import numpy as np
import ml_dtypes
from jax import lax
from jax.experimental import pallas as pl
from jax.experimental.pallas import tpu as pltpu
from jax.sharding import PartitionSpec as P

AXES = ("shot", "line")
DEVS = 128
ROWS = 512
NS = 2048
TAPS = 128
CAP = 8
PAIR = 2 * CAP
SLOTS = DEVS * PAIR
RCV = 128
CMP = 256
SRC = 4
WIN = 256
BLOCKS = NS // TAPS
ROWBLK = 256
step_size = 0.5
f32, bf16, i32 = jnp.float32, jnp.bfloat16, jnp.int32
NT = (((1,), (1,)), ((), ()))
MIB = 1024 * 1024


def split_pair(matrix):
    high = matrix.astype(ml_dtypes.bfloat16)
    low = (matrix - high.astype(np.float64)).astype(ml_dtypes.bfloat16)
    return high, low


def make_tables():
    angle = 2.0 * np.pi * (np.arange(TAPS) + 0.5) / WIN
    place = np.arange(WIN)
    phase = place[:, None] * angle[None, :]
    forward = np.concatenate([np.cos(phase), -np.sin(phase)], axis=1)
    inverse = forward.T / TAPS
    lag_phase = np.arange(TAPS)[:, None] * angle[None, :]
    even = 2.0 * np.cos(lag_phase)
    even[0] = 1.0
    d_pair = np.concatenate(split_pair(forward[:TAPS]), axis=0)
    e_pair = np.concatenate(split_pair(forward[TAPS:]), axis=0)
    i_pair = np.concatenate(split_pair(inverse[:, :TAPS]), axis=1)
    c_pair = np.concatenate(split_pair(even), axis=1)
    tail = np.concatenate(split_pair(inverse[:, TAPS:] @ forward[TAPS:]), axis=1)
    return dict(d=d_pair, e=e_pair, i=i_pair, c=c_pair, tail=tail)


def two(values):
    high = values.astype(bf16)
    low = (values - high.astype(f32)).astype(bf16)
    return high, low


def mm(a, b):
    return jnp.dot(a, b, preferred_element_type=f32)


def iota(shape, dim):
    return lax.broadcasted_iota(i32, shape, dim)


def as_bf16(mask):
    return mask.astype(f32).astype(bf16)


def fine_mm(values, pair):
    width = pair.shape[1] // 2
    high, low = two(values)
    both = mm(high, pair)
    return both[:, :width] + (both[:, width:] + mm(low, pair[:, :width]))


def fetch(hbm_refs, vmem_refs, sems):
    copies = [pltpu.make_async_copy(src, dst, sems.at[j])
              for j, (src, dst) in enumerate(zip(hbm_refs, vmem_refs))]
    for copy in copies:
        copy.start()
    return copies


def flag16(mask):
    return jnp.where(mask, jnp.ones(mask.shape, bf16), jnp.zeros(mask.shape, bf16))


def iota16(shape, dim):
    return lax.broadcasted_iota(jnp.int16, shape, dim)


def row16(row, count):
    tile = jnp.broadcast_to(row.astype(i32), (16, row.shape[1])).astype(jnp.int16)
    return jnp.concatenate([tile] * (count // 16), axis=0)


def plan_kernel(count_hbm, rterm_hbm, cterm_hbm, rhome_hbm, chome_hbm, traces_hbm, pay_ref, slot_ref,
                count_ref, rterm_ref, cterm_ref, rhome_ref, chome_ref, tbuf, sems):
    parts = [pl.ds(j * 128, 128) for j in range(4)]
    copies = fetch(
        [rterm_hbm, cterm_hbm, rhome_hbm, chome_hbm, count_hbm] + [traces_hbm.at[p] for p in parts],
        [rterm_ref, cterm_ref, rhome_ref, chome_ref, count_ref] + [tbuf.at[p] for p in parts], sems)
    earlier = flag16(iota16((128, 128), 0) < iota16((128, 128), 1))
    count_up = jnp.concatenate([earlier, jnp.ones((128, 128), bf16)], axis=1)

    def look_up(term, home, bits):
        high, low = term >> 7, term & 127
        halves = jnp.concatenate([home >> bits, home & (2 ** bits - 1)], axis=0)
        rows = home.shape[0]
        both = mm(halves.astype(f32).astype(bf16), flag16(iota16((128, ROWS), 0) == row16(low, 128)))
        pick_high = iota((rows, ROWS), 0) == high
        return (jnp.sum(jnp.where(pick_high, both[:rows], 0.0), axis=0, keepdims=True),
                jnp.sum(jnp.where(pick_high, both[rows:], 0.0), axis=0, keepdims=True))

    for copy in copies[:5]:
        copy.wait()
    r_owner, r_place = look_up(rterm_ref[...], rhome_ref[...], 7)
    c_owner, c_place = look_up(cterm_ref[...], chome_ref[...], 8)
    for copy in copies[5:]:
        copy.wait()
    line128 = iota16((DEVS, ROWS), 0)
    mine16 = [flag16(line128 == row16(owner, DEVS)) for owner in (r_owner, c_owner)]
    mine = jnp.concatenate(mine16, axis=0)
    owners = jnp.concatenate(
        [jnp.broadcast_to(r_owner, (DEVS, ROWS)), jnp.broadcast_to(c_owner, (DEVS, ROWS))], axis=0)
    here = owners == (iota((2 * DEVS, ROWS), 0) & (DEVS - 1)).astype(f32)
    past = jnp.zeros((2 * DEVS, 128), f32)
    ranks, powers = [], []
    for j in range(4):
        part = slice(j * 128, (j + 1) * 128)
        seen = mm(mine[:, part], count_up)
        before = jnp.where(here[:, part], seen[:, :128] + past, 0.0)
        past = past + seen[:, 128:]
        ranks.append(jnp.concatenate([jnp.sum(before[:DEVS], axis=0, keepdims=True),
                                      jnp.sum(before[DEVS:], axis=0, keepdims=True)], axis=0))
        total = jnp.zeros((128, 128), f32)
        for b in range(BLOCKS):
            x = tbuf[part, b * 128:(b + 1) * 128].astype(f32)
            total = total + x * x
        powers.append(jnp.sum(jnp.transpose(total), axis=0, keepdims=True))
    rank = jnp.concatenate(ranks, axis=1)
    r_rank, c_rank = rank[0:1], rank[1:2] + CAP
    live = (iota((1, ROWS), 1) < count_ref[:, 0:1]).astype(f32)
    power = jnp.concatenate(powers, axis=1) * live
    slot_ref[...] = jnp.concatenate(
        [r_owner * PAIR + r_rank, c_owner * PAIR + c_rank, live, power, jnp.zeros((4, ROWS), f32)],
        axis=0)
    p_high = power.astype(bf16).astype(f32)
    p_low = power - p_high
    line = iota((PAIR, ROWS), 0).astype(f32)

    def weights(rank, place):
        at = line == rank
        return jnp.concatenate(
            [jnp.where(at, row, 0.0) for row in (place, p_high, p_low)], axis=0).astype(bf16)

    pay_ref[...] = lax.dot_general(
        jnp.concatenate(mine16, axis=1),
        jnp.concatenate([weights(r_rank, r_place), weights(c_rank, c_place)], axis=1),
        NT, preferred_element_type=f32)


def pick_kernel(got_ref, rcv_ref, cmp_ref, out_hbm, out_ref, sems):
    pairs = [jnp.concatenate(two(t[...]), axis=1) for t in (rcv_ref, cmp_ref)]
    half = DEVS // 8
    saves = []
    for h in range(8):
        got = got_ref[h * half:(h + 1) * half, :PAIR].astype(i32)
        for side, pair in enumerate(pairs):
            lane = iota((half, pair.shape[0]), 1)
            pick = jnp.concatenate(
                [as_bf16(lane == got[:, s:s + 1]) for s in range(side * CAP, (side + 1) * CAP)], axis=0)
            both = mm(pick, pair)
            values = both[:, :TAPS] + both[:, TAPS:]
            for s in range(CAP):
                out_ref[pl.ds(h * half * PAIR + side * CAP + s, half, stride=PAIR), :] = (
                    values[s * half:(s + 1) * half])
        part = pl.ds(h * half * PAIR, half * PAIR)
        saves.append(pltpu.make_async_copy(out_ref.at[part], out_hbm.at[part], sems.at[h]))
        saves[-1].start()
    for save in saves:
        save.wait()


def lags_kernel(after_ref, traces_ref, targets_ref, e_ref, i_ref, c_ref,
                even_ref, base_ref, last_ref):
    e_pair = e_ref[...]
    sign = 1.0 - 2.0 * (iota((1, TAPS), 1) & 1).astype(f32)
    own = [jnp.zeros((ROWBLK, TAPS), f32)] * 2
    cross = [jnp.zeros((ROWBLK, TAPS), f32)] * 2
    back = None
    for b in range(BLOCKS):
        now = traces_ref[:, b * 128:(b + 1) * 128]
        goal = targets_ref[:, b * 128:(b + 1) * 128]
        u = mm(jnp.concatenate([now, now], axis=1), e_pair)
        v = mm(jnp.concatenate([goal, goal], axis=1), e_pair)
        ur, ui = u[:, :TAPS], u[:, TAPS:]
        vr, vi = v[:, :TAPS], v[:, TAPS:]
        xr, xi = (ur, ui) if b == 0 else (ur + back[0], ui + back[1])
        own = [own[0] + (xr * ur + xi * ui), own[1] + (xr * ui - xi * ur)]
        cross = [cross[0] + (xr * vr + xi * vi), cross[1] + (xr * vi - xi * vr)]
        back = -sign * ui, sign * ur
    i_pair = i_ref[...]
    even_ref[...] = fine_mm(fine_mm(jnp.concatenate(own, axis=1), i_pair), c_ref[...])
    base_ref[...] = fine_mm(jnp.concatenate(cross, axis=1), i_pair)
    last_ref[...] = jnp.concatenate(back, axis=1)


def books_kernel(got_ref, slot_ref, srcloc_ref, src_ref,
                 settle_ref, energy_ref, rcol_ref, ccol_ref, line_ref, shot_ref, scale_ref):
    got = jnp.concatenate([got_ref[...], jnp.zeros((DEVS, 128 - 3 * PAIR), f32)], axis=1)
    turned = jnp.transpose(got)[:3 * PAIR].astype(bf16)
    half = DEVS * CAP
    spread = as_bf16((iota((DEVS, half), 1) >> 3) == iota((DEVS, half), 0))
    wide = mm(turned, spread)
    here = iota((CAP, half), 0) == (iota((CAP, half), 1) & (CAP - 1))

    def line_of(values):
        return jnp.sum(jnp.where(here, values, 0.0), axis=0, keepdims=True)

    for side, (start, count) in enumerate(((0, RCV), (RCV, CMP))):
        row = side * CAP
        place = line_of(wide[row:row + CAP]).astype(i32)
        power = line_of(wide[PAIR + row:PAIR + row + CAP] + wide[2 * PAIR + row:2 * PAIR + row + CAP])
        for c in range(count // 128):
            part = slice(start + c * 128, start + (c + 1) * 128)
            hit = iota((128, half), 0) + c * 128 == place
            settle_ref[part, :] = as_bf16(hit)
            energy = jnp.sum(jnp.where(hit, power, 0.0), axis=1, keepdims=True)
            energy_ref[part, :] = jnp.broadcast_to(step_size / jnp.maximum(energy, 1.0), (128, 128))
    lines = jnp.concatenate(
        [slot_ref[...], srcloc_ref[...].astype(f32), jnp.zeros((128 - 9, ROWS), f32)], axis=0)
    src = src_ref[...]
    for j in range(4):
        part = slice(j * 128, (j + 1) * 128)
        col = jnp.transpose(lines[:, part])
        rcol_ref[part, :] = jnp.broadcast_to(col[:, 0:1].astype(i32), (128, 128)).astype(jnp.int16)
        ccol_ref[part, :] = jnp.broadcast_to(col[:, 1:2].astype(i32), (128, 128)).astype(jnp.int16)
        src_rows = jnp.zeros((128, TAPS), f32)
        for s in range(SRC):
            src_rows = jnp.where(col[:, 8:9] == float(s), src[s:s + 1, :], src_rows)
        shot_ref[part, :] = src_rows
    live = slot_ref[2:3, :] > 0.0
    for j, row in enumerate((slot_ref[0:1, :], slot_ref[1:2, :], srcloc_ref[...].astype(f32))):
        line_ref[16 * j:16 * (j + 1), :] = jnp.broadcast_to(
            jnp.where(live, row, -1.0).astype(i32), (16, ROWS)).astype(jnp.int16)
    mine = iota((8, ROWS), 0) == srcloc_ref[...]
    energy = jnp.sum(jnp.where(mine, slot_ref[3:4, :], 0.0), axis=1, keepdims=True)
    scale_ref[:8, :] = jnp.broadcast_to(step_size / jnp.maximum(energy, 1.0), (8, TAPS))
    scale_ref[8:, :] = jnp.concatenate([src, jnp.zeros((8 - SRC, TAPS), f32)], axis=0)


def one_hot16(at, first, second):
    ones = jnp.ones(at.shape, bf16)
    return jnp.where((at == first) | (at == second), ones, jnp.zeros(at.shape, bf16))


def grad_kernel(fetched_ref, *refs):
    hbm_refs, (out_ref, src_out_ref) = refs[:11], refs[11:13]
    vmem_refs, rows_ref, sems = refs[13:24], refs[24], refs[25]
    copies = fetch(hbm_refs, vmem_refs, sems)
    (rcol_ref, ccol_ref, shot_ref, d_ref, even_ref, last_ref, tail_ref, i_ref, base_ref,
     line_ref, scale_ref) = vmem_refs
    chunk = 512
    chunks = SLOTS // chunk
    lane = iota16((ROWS, 128), 1)
    for k in range(chunks):
        part = slice(k * chunk, (k + 1) * chunk)
        rows_ref[part, :] = jnp.concatenate(two(fetched_ref[part, :]), axis=1)
    for copy in copies[:2]:
        copy.wait()
    rcol, ccol = rcol_ref[...], ccol_ref[...]
    both = None
    for k in range(chunks):
        pick = jnp.concatenate(
            [one_hot16(lane + jnp.int16(k * chunk + j * 128), rcol, ccol) for j in range(chunk // 128)],
            axis=1)
        part = mm(pick, rows_ref[k * chunk:(k + 1) * chunk, :])
        both = part if k == 0 else both + part
    for copy in copies[2:]:
        copy.wait()
    mixed = (shot_ref[...] + (both[:, :TAPS] + both[:, TAPS:])).astype(bf16)
    h = mm(jnp.concatenate([mixed, mixed], axis=1), d_ref[...])
    hr, hi = h[:, :TAPS], h[:, TAPS:]
    xr, xi = last_ref[:, :TAPS], last_ref[:, TAPS:]
    past = jnp.concatenate([xr * hr - xi * hi, xr * hi + xi * hr], axis=1)
    m = fine_mm(past, tail_ref[...])
    mr, mi = m[:, :TAPS], m[:, TAPS:]
    even = even_ref[...]
    spectrum = jnp.concatenate(
        [even * hr - (xr * mr + xi * mi), even * hi - (xr * mi - xi * mr)], axis=1)
    grad = fine_mm(spectrum, i_ref[...]) - base_ref[...]
    rows = jnp.concatenate(two(grad), axis=1)
    first = jnp.concatenate([line_ref[:16, :]] * (chunk // 16), axis=0)
    second = jnp.concatenate([line_ref[16:32, :]] * (chunk // 16), axis=0)
    for k in range(chunks):
        at = iota16((chunk, ROWS), 0) + jnp.int16(k * chunk)
        both = mm(one_hot16(at, first, second), rows)
        out_ref[k * chunk:(k + 1) * chunk, :] = both[:, :TAPS] + both[:, TAPS:]
    both = mm(flag16(iota16((16, ROWS), 0) == line_ref[32:, :]), rows)
    src_out_ref[...] = scale_ref[8:8 + SRC, :] - ((both[:8, :TAPS] + both[:8, TAPS:])
                                                  * scale_ref[:8, :])[:SRC]


def settle_kernel(grads_ref, pick_ref, energy_ref, rcv_ref, cmp_ref, src_ref,
                  src_out_ref, rcv_out_ref, cmp_out_ref):
    src_out_ref[...] = src_ref[...]
    sides = grads_ref[...].reshape(DEVS, 2, CAP, TAPS)
    for side, part, table_ref, out_ref in ((0, slice(0, RCV), rcv_ref, rcv_out_ref),
                                           (1, slice(RCV, RCV + CMP), cmp_ref, cmp_out_ref)):
        rows = jnp.concatenate(two(sides[:, side].reshape(DEVS * CAP, TAPS)), axis=1)
        total = mm(pick_ref[part, :], rows)
        out_ref[...] = table_ref[...] - (total[:, :TAPS] + total[:, TAPS:]) * energy_ref[part, :]


def shape(*dims, dtype=f32):
    return jax.ShapeDtypeStruct(dims, dtype)


VM = pl.BlockSpec(memory_space=pltpu.VMEM)
HB = pl.BlockSpec(memory_space=pltpu.HBM)
DMA = pltpu.SemaphoreType.DMA
small = pltpu.CompilerParams(vmem_limit_bytes=24 * MIB)
large = pltpu.CompilerParams(vmem_limit_bytes=60 * MIB + MIB // 2)


def whole(array):
    return pl.BlockSpec(array.shape, lambda i: (0,) * len(array.shape))


def in_hbm(*arrays):
    return [pltpu.with_memory_space_constraint(a, pltpu.HBM) for a in arrays]


def hbm(*dims, dtype=f32):
    return pltpu.HBM(dims, dtype)


def vmem(*dims, dtype=f32):
    return pltpu.VMEM(dims, dtype)


def run_plan(traces, rcv_term, cmp_term, rcv_home, cmp_home, counts):
    args = in_hbm(rcv_term.reshape(1, ROWS), cmp_term.reshape(1, ROWS),
                  rcv_home.reshape(-1, 128), cmp_home.reshape(-1, 128), traces)
    return pl.pallas_call(
        plan_kernel,
        out_shape=(vmem(DEVS, 3 * PAIR), vmem(8, ROWS)),
        in_specs=[HB] * 6,
        out_specs=(VM, VM),
        scratch_shapes=[vmem(1, 128, dtype=i32), vmem(1, ROWS, dtype=i32), vmem(1, ROWS, dtype=i32),
                        vmem(128, 128, dtype=i32), vmem(256, 128, dtype=i32),
                        vmem(ROWS, NS, dtype=bf16), DMA((9,))],
        compiler_params=small,
        name="plan",
    )(*in_hbm(jnp.pad(counts, (0, 127)).reshape(1, 128)), *args)


def run_pick(got, rcv_filters, cmp_filters):
    return pl.pallas_call(
        pick_kernel,
        out_shape=hbm(SLOTS, TAPS),
        in_specs=[VM] * 3, out_specs=HB,
        scratch_shapes=[vmem(SLOTS + DEVS, TAPS), DMA((8,))],
        compiler_params=small,
        name="pick",
    )(got, rcv_filters, cmp_filters)


def run_lags(got, traces, targets, tables):
    def blk(width):
        return pl.BlockSpec((ROWBLK, width), lambda i: (i, 0))

    return pl.pallas_call(
        lags_kernel,
        grid=(ROWS // ROWBLK,),
        out_shape=(hbm(ROWS, TAPS), hbm(ROWS, TAPS), hbm(ROWS, WIN)),
        in_specs=[pl.BlockSpec((8, 3 * PAIR), lambda i: (0, 0)), blk(NS), blk(NS)]
        + [whole(tables[n]) for n in "eic"],
        out_specs=(blk(TAPS), blk(TAPS), blk(WIN)),
        compiler_params=large,
        cost_estimate=pl.CostEstimate(flops=5 * 10 ** 9, bytes_accessed=5 * 10 ** 6,
                                      transcendentals=0),
        name="lags",
    )(*in_hbm(got, traces, targets, *[tables[n] for n in "eic"]))


def run_books(got, slot_lines, src_line, src_filters):
    int16 = jnp.int16
    out = (hbm(RCV + CMP, DEVS * CAP, dtype=bf16), hbm(RCV + CMP, TAPS),
           hbm(ROWS, TAPS, dtype=int16), hbm(ROWS, TAPS, dtype=int16),
           hbm(48, ROWS, dtype=int16), hbm(ROWS, TAPS), hbm(16, TAPS))
    args = (got, slot_lines, src_line, src_filters)
    return pl.pallas_call(
        books_kernel,
        grid=(1,),
        out_shape=out,
        in_specs=[whole(a) for a in args], out_specs=[whole(a) for a in out],
        compiler_params=large,
        name="books",
    )(got, slot_lines, *in_hbm(*args[2:]))


def run_grad(fetched, held):
    return pl.pallas_call(
        grad_kernel,
        out_shape=(vmem(SLOTS, TAPS), vmem(SRC, TAPS)),
        in_specs=[VM] + [HB] * len(held), out_specs=(VM, VM),
        scratch_shapes=[vmem(*a.shape, dtype=a.dtype) for a in held]
        + [vmem(SLOTS, 2 * TAPS, dtype=bf16), DMA((len(held),))],
        compiler_params=small,
        name="grad",
    )(pltpu.with_memory_space_constraint(fetched, pltpu.VMEM), *in_hbm(*held))


def run_settle(back, settle_pick, energy, rcv_filters, cmp_filters, src_new):
    return pl.pallas_call(
        settle_kernel,
        out_shape=(shape(SRC, TAPS), shape(RCV, TAPS), shape(CMP, TAPS)),
        in_specs=[VM] * 6, out_specs=(VM, VM, VM),
        compiler_params=small,
        name="settle",
    )(back, settle_pick, energy, rcv_filters, cmp_filters, src_new)


def swap(rows):
    return lax.all_to_all(rows.reshape(DEVS, PAIR, TAPS), AXES, split_axis=0, concat_axis=0,
                          tiled=True).reshape(SLOTS, TAPS)


def body(traces, targets, src_local, rcv_term, cmp_term, rcv_home, cmp_home, counts,
         src_filters, rcv_filters, cmp_filters):
    tables = {name: jnp.asarray(value) for name, value in make_tables().items()}
    src_line = src_local.reshape(1, ROWS)
    pay, slot_lines = run_plan(traces, rcv_term, cmp_term, rcv_home, cmp_home, counts)
    got = lax.all_to_all(pay, AXES, split_axis=0, concat_axis=0, tiled=True)
    fetched = swap(run_pick(got, rcv_filters, cmp_filters))
    even, base, last = run_lags(got, traces, targets, tables)
    settle_pick, energy, rcol, ccol, lines, shots, scale = run_books(
        got, slot_lines, src_line, src_filters)
    send, src_new = run_grad(fetched, (rcol, ccol, shots, tables["d"], even, last, tables["tail"],
                                       tables["i"], base, lines, scale))
    return run_settle(swap(send), settle_pick, energy, rcv_filters, cmp_filters, src_new)


def solution(mesh):
    rows = P(AXES, None)
    flat = P(AXES)
    return jax.shard_map(
        body,
        mesh=mesh,
        in_specs=(rows, rows, flat, flat, flat, P(), P(), flat, rows, rows, rows),
        out_specs=(rows, rows, rows),
        check_vma=False,
    )
```
